32 devices in a mesh: replica: 8 (over y, x, core), fsdp: 4 (over z).
Axes of the slice: x: 2, y: 2, z: 4, core: 2. Of those that a mesh axis runs over, the one named last changes fastest.
Arguments:
- hidden: bfloat16 [8, 2, 256, 8192], P('replica', None, 'fsdp'), may hold values from -6 to 6
- targets: bfloat16 [8, 2, 256, 512], P('replica', None, 'fsdp'), may hold values from -16 to 16
- doc_ids: int32 [8, 2, 256], P('replica', None, 'fsdp'), may hold values from 0 to 7, never falling along the last dimension, each value on 1 to 64 neighbouring positions
- weights: bfloat16 [8, 8192, 512], P('replica', 'fsdp'), may hold values from -5 to 5
- adam_m: bfloat16 [8, 8192, 512], P('replica', 'fsdp'), may hold values from -1.335144e-05 to 1.335144e-05
- adam_v: bfloat16 [8, 8192, 512], P('replica', 'fsdp'), may hold values from 3.623768e-13 to 3.6379788e-11
- anchor: bfloat16 [8192, 128], P('fsdp'), may hold values from -5 to 5
- momentum: bfloat16 [8192, 128], P('fsdp'), may hold values from -5 to 5
- fragment: int32 [1], replicated, may hold values from 0 to 3
Outputs:
- new_weights: float32 [8, 8192, 512], P('replica', 'fsdp')
- losses: float32 [8, 2], P('replica')
The draws below stay inside these ranges and needn't reach their ends.
Inputs may be any that keep to these rules, and one draw needn't show every extreme that they name: `doc_ids`: in each row (replica, step) the document numbers never fall, every number 0 to 7 occurs, each document has 1 to 64 tokens and one has exactly 64.
All inputs are finite; a program needn't handle non-finite values.
Results may differ from the reference program's by a relative error of at most 0.0003.
Values may be sent and summed in bfloat16 or wider, within the bound.
A program may use at most 64 MiB of HBM per device.

```python
import math
import jax
import jax.numpy as jnp
import numpy as np
from jax import lax

D = 8192
WV = 512
FRAGS = 4
FW = 128
STEPS = 2
DOCS = 8
TOKENS = 256
DOC_MOST = 64
N_REPLICA = 8


def draw_targets(key, part):
    key = jax.random.fold_in(key, 11)
    first_key, second_key = jax.random.split(key, 2)
    shape = (N_REPLICA, STEPS, TOKENS, WV)
    base = jax.random.truncated_normal(first_key, -4.0, 4.0, shape, jnp.float32)
    spread = jnp.exp(jax.random.uniform(second_key, (N_REPLICA, STEPS, TOKENS, 1), jnp.float32, math.log(0.3), math.log(3.0)))
    return (base * spread).astype(jnp.bfloat16)


def steps_of(own_key, dims, cuts, smallest, high):
    gain = 1.0
    for axis_at, shards_of in cuts:
        draws = jax.random.uniform(jax.random.fold_in(jax.random.fold_in(own_key, 6), axis_at), (shards_of,), jnp.float32, smallest / len(cuts), high / len(cuts))
        gain = gain * jnp.repeat(jnp.exp(draws), dims[axis_at] // shards_of).reshape((-1,) + (1,) * (len(dims) - 1 - axis_at))
    return gain


def split_up(count, total, most, slope):
    portions = [(1 << 20) // math.isqrt(rank ** slope) + 1 for rank in range(2, count + 1)]
    rest, given = total - most - (count - 1), [1] * (count - 1)
    while rest > 0:
        candidates = [i for i in range(count - 1) if given[i] < most]
        whole, budget = sum([portions[i] for i in candidates]), rest
        for i in candidates:
            addition = min(most - given[i], max(1, budget * portions[i] // whole), rest)
            given[i] = given[i] + addition
            rest = rest - addition
    return np.array([most] + given)


def uneven(own_key, count, total, limit, lean):
    if count == 2:
        one = jax.random.randint(own_key, (), max(1, total - limit), min(limit, total - 1) + 1)
        return jnp.stack([one, total - one])
    sizes = jnp.asarray(split_up(count, total, limit, lean), jnp.int32)
    pairs = (count - 1) // 2
    source_of, taker = sizes[1:1 + 2 * pairs:2], sizes[2:2 + 2 * pairs:2]
    room = jnp.minimum(source_of - 1, limit - taker)
    moved = jax.random.randint(jax.random.fold_in(own_key, 1), (pairs,), 0, 1 << 20) % (room + 1)
    sizes = sizes.at[1:1 + 2 * pairs:2].set(source_of - moved).at[2:2 + 2 * pairs:2].set(taker + moved)
    return sizes[jax.random.permutation(jax.random.fold_in(own_key, 2), count)]


def noise(key, extent, scale, most, cuts=(), held_as=jnp.bfloat16):
    values = scale * jax.random.normal(key, extent, jnp.float32)
    if cuts:
        values = values * steps_of(key, extent, cuts, -0.22, 0.18)
    return jnp.clip(values, -most, most).astype(held_as)


def setup_inputs(seed: int = 0) -> dict:
    key_list = jax.random.split(jax.random.key(seed), 10)
    return {
        "hidden": noise(key_list[0], (N_REPLICA, STEPS, TOKENS, D), 1.0, 6.0, ((0, 8), (2, 4))),
        "targets": draw_targets(jax.random.fold_in(key_list[9], 71), 0),
        "doc_ids": jax.vmap(lambda own: jnp.searchsorted(jnp.cumsum(uneven(own, DOCS, TOKENS, DOC_MOST, 1)), jnp.arange(TOKENS), side="right"))(jax.random.split(key_list[2], N_REPLICA * STEPS)).reshape((N_REPLICA, STEPS, TOKENS)).astype(jnp.int32),
        "weights": noise(key_list[3], (N_REPLICA, D, WV), 1.0, 5.0, ((0, 8), (1, 4))),
        "adam_m": noise(key_list[4], (N_REPLICA, D, WV), (0.7 / (WV * (D * TOKENS) ** 0.5)), 1.33514404296875e-05, ((0, 8), (1, 4))),
        "adam_v": jnp.clip(jnp.exp(math.log(3.637978807091713e-11) - 4.609084 * jax.random.uniform(key_list[5], (N_REPLICA, D, WV), jnp.float32) ** steps_of(key_list[5], (N_REPLICA, D, WV), ((0, 8), (1, 4)), -0.2, 0.2)), 3.623767952376511e-13, 3.637978807091713e-11).astype(jnp.bfloat16),
        "anchor": noise(key_list[6], (D, FW), 1.0, 5.0, ((0, 4),)),
        "momentum": noise(key_list[7], (D, FW), 1.0, 5.0, ((0, 4),)),
        "fragment": jax.random.randint(key_list[8], (1,), 0, FRAGS).astype(jnp.int32),
    }


NORM_EPS = 1e-05
ADAM_EPS = 1e-08
INNER_RATE = 0.1
DECAY_RATE = 0.1
BETA_FIRST = 0.9
BETA_SECOND = 0.95
OUTER_RATE = 0.7
NESTEROV = 0.9
MIXING = 0.5

def normalize(block):
    wide = block.astype(jnp.float32)
    power = lax.optimization_barrier(jnp.mean(wide * wide, axis=-1, keepdims=True))
    return (wide * lax.rsqrt(power + NORM_EPS)).astype(jnp.bfloat16)

def token_weights(labels):
    onehot = (labels[:, None] == jnp.arange(DOCS, dtype=jnp.int32)[None, :]).astype(jnp.float32)
    counts = lax.optimization_barrier(jnp.sum(onehot, axis=0))
    inverse = 1.0 / (DOCS * counts)
    return jnp.dot(onehot, inverse, precision=lax.Precision.HIGHEST)

def adam_update(master, first, second, gradient):
    first = BETA_FIRST * first + (1.0 - BETA_FIRST) * gradient
    second = BETA_SECOND * second + (1.0 - BETA_SECOND) * gradient * gradient
    master = master - INNER_RATE * (first / (jnp.sqrt(second) + ADAM_EPS) + DECAY_RATE * master)
    return (master, first, second)

def reference(hidden, targets, doc_ids, weights, adam_m, adam_v, anchor, momentum, fragment):
    zero = jnp.zeros((), jnp.int32)
    start = (fragment[0] * FW).astype(jnp.int32)
    local = lax.dynamic_slice(weights, (zero, zero, start), (N_REPLICA, D, FW))
    delta = anchor.astype(jnp.float32)[None] - local.astype(jnp.float32)
    mean_delta = lax.optimization_barrier(jnp.sum(delta, axis=0)) / N_REPLICA
    new_momentum = NESTEROV * momentum.astype(jnp.float32) + mean_delta
    global_fragment = anchor.astype(jnp.float32) - OUTER_RATE * (mean_delta + NESTEROV * new_momentum)
    scale = D ** (-0.5)

    def replica(packed):
        hidden_rows, target_rows, label_rows, weight_rows, first_rows, second_rows = packed
        master = weight_rows.astype(jnp.float32)
        first = first_rows.astype(jnp.float32)
        second = second_rows.astype(jnp.float32)
        step_losses = []
        for step_index in range(STEPS):
            normed = normalize(hidden_rows[step_index])
            current = master.astype(jnp.bfloat16)
            values = jnp.dot(normed, current, preferred_element_type=jnp.float32) * scale
            error = values - target_rows[step_index].astype(jnp.float32)
            weight_row = token_weights(label_rows[step_index])
            step_losses.append(jnp.sum(weight_row * 0.5 * lax.optimization_barrier(jnp.mean(error * error, axis=-1))))
            error_grad = (weight_row[:, None] * error / WV).astype(jnp.bfloat16)
            gradient = jnp.dot(normed.T, error_grad, preferred_element_type=jnp.float32) * scale
            master, first, second = adam_update(master, first, second, gradient)
        merged = MIXING * lax.dynamic_slice(master, (zero, start), (D, FW)) + (1.0 - MIXING) * global_fragment
        master = lax.dynamic_update_slice(master, merged, (zero, start))
        return (master, jnp.stack(step_losses))
    new_weights, losses = lax.map(replica, (hidden, targets, doc_ids, weights, adam_m, adam_v))
    return (new_weights, losses)
```

```python
import functools

import jax
import jax.numpy as jnp
from jax import lax
from jax.experimental import pallas as pl
from jax.experimental.pallas import tpu as pltpu
from jax.sharding import PartitionSpec as P

DOCS = 8
NORM_EPS = 1e-05
ADAM_EPS = 1e-08
INNER_RATE = 0.1
DECAY_RATE = 0.1
BETA_FIRST = 0.9
BETA_SECOND = 0.95
OUTER_RATE = 0.7
NESTEROV = 0.9
MIXING = 0.5
LANES = 128
MESH = pl.DeviceIdType.MESH
F32 = jnp.float32
BF16 = jnp.bfloat16


def adam_update(master, first, second, gradient):
    first = BETA_FIRST * first + (1.0 - BETA_FIRST) * gradient
    second = BETA_SECOND * second + (1.0 - BETA_SECOND) * gradient * gradient
    master = master - INNER_RATE * (first / (jnp.sqrt(second) + ADAM_EPS) + DECAY_RATE * master)
    return (master, first, second)


def partners(me, n):
    if n == 4:
        return [lax.rem(me + 2, 4), 3 - me, me + 1 - 2 * lax.rem(me, 2)]
    return [lax.rem(me + k, n) for k in range(1, n)]


def window_kernel(
    n, replicas, dims,
    hidden, targets, doc_ids, weights, adam_m, adam_v, anchor, momentum, fragment,
    master_out, first_out, second_out, turned_out, grads_out, frag_out, loss_out,
    cols, hid, w_ref, m_ref, v_ref, current, master, first, second, turned,
    partial, part_send, part_recv, grads, counts, losses,
    frag_cols, frag_recv, frag_all, anchor_ref, moment_ref, row_scale, token_weight,
    local_sem, out_sem, a2a_send, a2a_recv, count_send, count_recv,
    frag_send, frag_got, all_send, all_got, part_send_sem, part_recv_sem,
    grad_send, grad_recv, loss_send, loss_recv,
):
    steps, tokens, rows, width, model, fw = dims
    own = rows // replicas
    scale = model ** (-0.5)
    rep = lax.axis_index("replica")
    me = lax.axis_index("fsdp")
    others = partners(me, n)
    peers = [lax.rem(rep + k, replicas) for k in range(1, replicas)]

    def block(index, size):
        return pl.ds(pl.multiple_of(index * size, size), size)

    my_tokens = block(me, tokens)
    my_frag = block(rep, own)

    local = [
        pltpu.make_async_copy(weights.at[0], w_ref, local_sem.at[0]),
        pltpu.make_async_copy(hidden.at[0], hid, local_sem.at[1]),
        pltpu.make_async_copy(anchor.at[my_frag, :], anchor_ref, local_sem.at[2]),
        pltpu.make_async_copy(momentum.at[my_frag, :], moment_ref, local_sem.at[3]),
        pltpu.make_async_copy(adam_m.at[0], m_ref, local_sem.at[4]),
        pltpu.make_async_copy(adam_v.at[0], v_ref, local_sem.at[5]),
    ]
    for s in range(steps):
        local.append(pltpu.make_async_copy(
            hidden.at[0, s, :, block(me, rows)], cols.at[s, my_tokens, :], local_sem.at[6 + s]))
    for copy in local:
        copy.start()

    barrier = pltpu.get_barrier_semaphore()
    for j in others:
        pl.semaphore_signal(barrier, inc=1, device_id=(rep, j), device_id_type=MESH)
    for i in peers:
        pl.semaphore_signal(barrier, inc=1, device_id=(i, me), device_id_type=MESH)
    pl.semaphore_wait(barrier, n + replicas - 2)

    def a2a(s, j):
        return pltpu.make_async_remote_copy(
            src_ref=hidden.at[0, s, :, block(j, rows)], dst_ref=cols.at[s, my_tokens, :],
            send_sem=a2a_send.at[s, j], recv_sem=a2a_recv.at[s, me],
            device_id=(rep, j), device_id_type=MESH)

    def a2a_arrived(s, j):
        pltpu.make_async_remote_copy(
            src_ref=hidden.at[0, s, :, block(j, rows)], dst_ref=cols.at[s, block(j, tokens), :],
            send_sem=a2a_send.at[s, j], recv_sem=a2a_recv.at[s, j],
            device_id=(rep, j), device_id_type=MESH).wait_recv()

    for j in others:
        a2a(0, j).start()

    lane = lax.broadcasted_iota(jnp.int32, (tokens, LANES), 1).astype(F32)
    eye = (lax.broadcasted_iota(jnp.int32, (tokens, tokens), 0)
           == lax.broadcasted_iota(jnp.int32, (tokens, tokens), 1))
    onehots = []
    row8 = lax.broadcasted_iota(jnp.int32, (8, LANES), 0)
    tally = jnp.zeros((8, LANES), F32)
    for s in range(steps):
        ids = jnp.broadcast_to(doc_ids[0, s:s + 1, :].astype(F32), (tokens, tokens))
        ids = jnp.sum(jnp.where(eye, ids, 0.0), axis=1, keepdims=True)
        onehot = (ids == lane).astype(F32)
        onehots.append(onehot)
        tally = tally + jnp.where(row8 == s, jnp.sum(onehot, axis=0, keepdims=True), 0.0)
    counts[me] = tally

    def to_all(buf, send, recv, j):
        return pltpu.make_async_remote_copy(
            src_ref=buf.at[me], dst_ref=buf.at[me], send_sem=send.at[j], recv_sem=recv.at[me],
            device_id=(rep, j), device_id_type=MESH)

    def from_all(buf, send, recv, j):
        pltpu.make_async_remote_copy(
            src_ref=buf.at[j], dst_ref=buf.at[j], send_sem=send.at[j], recv_sem=recv.at[j],
            device_id=(rep, j), device_id_type=MESH).wait_recv()

    for j in others:
        to_all(counts, count_send, count_recv, j).start()

    local[0].wait()
    picked = fragment[0]
    for k in range(width // fw):
        piece = w_ref[:, k * fw:(k + 1) * fw]
        if k == 0:
            frag_cols[...] = piece
        else:
            frag_cols[...] = jnp.where(picked == k, piece, frag_cols[...])

    def frag_copy(i):
        return pltpu.make_async_remote_copy(
            src_ref=frag_cols.at[block(i, own), :], dst_ref=frag_recv.at[rep],
            send_sem=frag_send.at[i], recv_sem=frag_got.at[rep],
            device_id=(i, me), device_id_type=MESH)

    for i in peers:
        frag_copy(i).start()
    frag_recv[rep] = frag_cols[my_frag, :]

    local[1].wait()
    wide = 4 * LANES
    for s in range(steps):
        def add_squares(c, acc, s=s):
            x = hid[s, :, block(c, wide)].astype(F32)
            return acc + x * x
        acc = lax.fori_loop(0, model // wide, add_squares, jnp.zeros((tokens, wide), F32))
        power = jnp.sum(acc, axis=1, keepdims=True) / model
        row_scale[s] = jnp.broadcast_to(lax.rsqrt(power + NORM_EPS), (tokens, LANES))

    for j in others:
        from_all(counts, count_send, count_recv, j)
    total = counts[0]
    for j in range(1, n):
        total = total + counts[j]
    inverse = jnp.where(total > 0.0, 1.0 / (DOCS * jnp.maximum(total, 1.0)), 0.0)
    for s in range(steps):
        weight = jnp.sum(onehots[s] * inverse[s:s + 1, :], axis=1, keepdims=True)
        token_weight[s] = jnp.broadcast_to(weight, (tokens, LANES))

    for i in peers:
        pltpu.make_async_remote_copy(
            src_ref=frag_recv.at[i], dst_ref=frag_recv.at[i], send_sem=frag_send.at[i],
            recv_sem=frag_got.at[i], device_id=(i, me), device_id_type=MESH).wait_recv()
    local[2].wait()
    local[3].wait()
    base = anchor_ref[...].astype(F32)
    delta = base - frag_recv[0].astype(F32)
    for i in range(1, replicas):
        delta = delta + (base - frag_recv[i].astype(F32))
    mean_delta = delta / replicas
    new_moment = NESTEROV * moment_ref[...].astype(F32) + mean_delta
    frag_all[my_frag, :] = base - OUTER_RATE * (mean_delta + NESTEROV * new_moment)

    def all_copy(i):
        return pltpu.make_async_remote_copy(
            src_ref=frag_all.at[my_frag, :], dst_ref=frag_all.at[my_frag, :],
            send_sem=all_send.at[i], recv_sem=all_got.at[rep],
            device_id=(i, me), device_id_type=MESH)

    for i in peers:
        all_copy(i).start()

    for j in others:
        a2a(0, j).wait_send()
        a2a(1, j).start()

    def part_copy(s, j):
        return pltpu.make_async_remote_copy(
            src_ref=part_send.at[s, block(j, tokens), :], dst_ref=part_recv.at[s, me],
            send_sem=part_send_sem.at[s, j], recv_sem=part_recv_sem.at[s, me],
            device_id=(rep, j), device_id_type=MESH)

    def grad_copy(s, j):
        return pltpu.make_async_remote_copy(
            src_ref=grads.at[s, my_tokens, :], dst_ref=grads.at[s, my_tokens, :],
            send_sem=grad_send.at[s, j], recv_sem=grad_recv.at[s, me],
            device_id=(rep, j), device_id_type=MESH)

    tile = 256

    def project_and_share(s, held):
        for j in others:
            a2a_arrived(s, j)
        local[6 + s].wait()

        @pl.loop(0, width // tile)
        def _(c):
            at = block(c, tile)
            out = jnp.dot(cols[s], held[:, at], preferred_element_type=F32)
            partial[:, at] = out
            part_send[s, :, at] = out.astype(BF16)

        for j in others:
            part_copy(s, j).start()

        @pl.loop(0, rows // tile)
        def _(c):
            at = block(c, tile)
            turned[s, at, :] = cols[s, :, at].T

        values = partial[my_tokens, :]
        for j in others:
            pltpu.make_async_remote_copy(
                src_ref=part_recv.at[s, j], dst_ref=part_recv.at[s, j],
                send_sem=part_send_sem.at[s, j], recv_sem=part_recv_sem.at[s, j],
                device_id=(rep, j), device_id_type=MESH).wait_recv()
            values = values + part_recv[s, j].astype(F32)
        gain = row_scale[s][:, :1]
        weight = token_weight[s][:, :1]
        error = values * (gain * scale) - targets[0, s].astype(F32)
        grads[s, my_tokens, :] = ((weight * gain / width) * error).astype(BF16)
        for j in others:
            grad_copy(s, j).start()
        loss = jnp.sum(weight * 0.5 * jnp.mean(error * error, axis=-1, keepdims=True))
        loss = jnp.where(row8 == s, loss, 0.0)
        if s == 0:
            losses[me] = loss
        else:
            losses[me] = losses[me] + loss
        if s == steps - 1:
            for j in others:
                to_all(losses, loss_send, loss_recv, j).start()
        for j in others:
            pltpu.make_async_remote_copy(
                src_ref=grads.at[s, block(j, tokens), :], dst_ref=grads.at[s, block(j, tokens), :],
                send_sem=grad_send.at[s, j], recv_sem=grad_recv.at[s, j],
                device_id=(rep, j), device_id_type=MESH).wait_recv()

    project_and_share(0, w_ref)
    local[4].wait()
    local[5].wait()
    rt = 128

    @pl.loop(0, rows // rt)
    def _(c):
        at = block(c, rt)
        gradient = jnp.dot(turned[0, at, :], grads[0], preferred_element_type=F32) * scale
        new_master, new_first, new_second = adam_update(
            w_ref[at, :].astype(F32), m_ref[at, :].astype(F32), v_ref[at, :].astype(F32), gradient)
        master[at, :] = new_master
        first[at, :] = new_first
        second[at, :] = new_second
        current[at, :] = new_master.astype(BF16)

    outs = [
        pltpu.make_async_copy(master, master_out, out_sem.at[0]),
        pltpu.make_async_copy(first, first_out, out_sem.at[1]),
        pltpu.make_async_copy(second, second_out, out_sem.at[2]),
    ]
    for copy in outs:
        copy.start()
    for i in peers:
        at = block(i, own)
        pltpu.make_async_remote_copy(
            src_ref=frag_all.at[at, :], dst_ref=frag_all.at[at, :], send_sem=all_send.at[i],
            recv_sem=all_got.at[i], device_id=(i, me), device_id_type=MESH).wait_recv()
    outs.append(pltpu.make_async_copy(frag_all, frag_out, out_sem.at[3]))
    outs[-1].start()

    project_and_share(1, current)
    outs.append(pltpu.make_async_copy(turned.at[1], turned_out, out_sem.at[4]))
    outs.append(pltpu.make_async_copy(grads.at[1], grads_out, out_sem.at[5]))
    outs[-2].start()
    outs[-1].start()
    for j in others:
        from_all(losses, loss_send, loss_recv, j)
    loss = losses[0]
    for j in range(1, n):
        loss = loss + losses[j]
    loss_out[...] = loss

    for j in others:
        a2a(1, j).wait_send()
        to_all(counts, count_send, count_recv, j).wait_send()
        to_all(losses, loss_send, loss_recv, j).wait_send()
        for s in range(steps):
            part_copy(s, j).wait_send()
            grad_copy(s, j).wait_send()
    for i in peers:
        frag_copy(i).wait_send()
        all_copy(i).wait_send()
    for copy in outs:
        copy.wait()


def finish_kernel(scale, fw, fragment, master, first, second, turned, grads, frag, loss,
                  out, loss_out):
    gradient = jnp.dot(turned[...], grads[...], preferred_element_type=F32) * scale
    new_master, _, _ = adam_update(master[...], first[...], second[...], gradient)
    picked = fragment[0]
    mixed = (1.0 - MIXING) * frag[...]
    for k in range(out.shape[2] // fw):
        piece = new_master[:, k * fw:(k + 1) * fw]
        out[0, :, k * fw:(k + 1) * fw] = jnp.where(picked == k, MIXING * piece + mixed, piece)
    steps = loss_out.shape[1]
    across = lax.broadcasted_iota(jnp.int32, (1, steps), 1)
    line = jnp.zeros((1, steps), F32)
    for s in range(steps):
        line = jnp.where(across == s, loss[s:s + 1, :steps], line)
    loss_out[...] = line


def body(n, replicas, hidden, targets, doc_ids, weights, adam_m, adam_v, anchor, momentum, fragment):
    steps, tokens, model = hidden.shape[1:]
    rows, width = weights.shape[1:]
    fw = anchor.shape[1]
    own = rows // replicas
    everyone = n * tokens
    dims = (steps, tokens, rows, width, model, fw)
    any_spec = pl.BlockSpec(memory_space=pl.ANY)
    vmem = pl.BlockSpec(memory_space=pltpu.VMEM)
    smem = pl.BlockSpec(memory_space=pltpu.SMEM)
    dma = pltpu.SemaphoreType.DMA
    shape = jax.ShapeDtypeStruct
    master, first, second, turned, grads, frag, loss = pl.pallas_call(
        functools.partial(window_kernel, n, replicas, dims),
        out_shape=[
            shape((rows, width), F32), shape((rows, width), F32), shape((rows, width), F32),
            shape((rows, everyone), BF16), shape((everyone, width), BF16),
            shape((rows, fw), F32), shape((8, LANES), F32),
        ],
        in_specs=[any_spec, vmem, vmem, any_spec, any_spec, any_spec, any_spec, any_spec, smem],
        out_specs=[any_spec] * 6 + [vmem],
        scratch_shapes=[
            pltpu.VMEM((steps, everyone, rows), BF16),
            pltpu.VMEM((steps, tokens, model), BF16),
            pltpu.VMEM((rows, width), BF16),
            pltpu.VMEM((rows, width), BF16),
            pltpu.VMEM((rows, width), BF16),
            pltpu.VMEM((rows, width), BF16),
            pltpu.VMEM((rows, width), F32),
            pltpu.VMEM((rows, width), F32),
            pltpu.VMEM((rows, width), F32),
            pltpu.VMEM((steps, rows, everyone), BF16),
            pltpu.VMEM((everyone, width), F32),
            pltpu.VMEM((steps, everyone, width), BF16),
            pltpu.VMEM((steps, n, tokens, width), BF16),
            pltpu.VMEM((steps, everyone, width), BF16),
            pltpu.VMEM((n, 8, LANES), F32),
            pltpu.VMEM((n, 8, LANES), F32),
            pltpu.VMEM((rows, fw), BF16),
            pltpu.VMEM((replicas, own, fw), BF16),
            pltpu.VMEM((rows, fw), F32),
            pltpu.VMEM((own, fw), BF16),
            pltpu.VMEM((own, fw), BF16),
            pltpu.VMEM((steps, tokens, LANES), F32),
            pltpu.VMEM((steps, tokens, LANES), F32),
            dma((6 + steps,)), dma((6,)),
            dma((steps, n)), dma((steps, n)), dma((n,)), dma((n,)),
            dma((replicas,)), dma((replicas,)), dma((replicas,)), dma((replicas,)),
            dma((steps, n)), dma((steps, n)),
            dma((steps, n)), dma((steps, n)), dma((n,)), dma((n,)),
        ],
        compiler_params=pltpu.CompilerParams(
            collective_id=0, has_side_effects=True, vmem_limit_bytes=52 * 1024 * 1024),
        name="window",
    )(hidden, targets, doc_ids, weights, adam_m, adam_v, anchor, momentum, fragment)

    rt = min(256, rows)
    whole = lambda shape: pl.BlockSpec(shape, lambda i: (0, 0))
    piece = lambda cols: pl.BlockSpec((rt, cols), lambda i: (i, 0))
    return pl.pallas_call(
        functools.partial(finish_kernel, model ** (-0.5), fw),
        grid=(rows // rt,),
        out_shape=[shape((1, rows, width), F32), shape((1, steps), F32)],
        in_specs=[smem, piece(width), piece(width), piece(width), piece(everyone),
                  whole((everyone, width)), piece(fw), whole((8, LANES))],
        out_specs=[pl.BlockSpec((1, rt, width), lambda i: (0, i, 0)), whole((1, steps))],
        compiler_params=pltpu.CompilerParams(vmem_limit_bytes=32 * 1024 * 1024),
        name="finish",
    )(fragment, master, first, second, turned, grads, frag, loss)


def solution(mesh):
    placed = (
        P("replica", None, "fsdp", None),
        P("replica", None, "fsdp", None),
        P("replica", None, "fsdp"),
        P("replica", "fsdp", None),
        P("replica", "fsdp", None),
        P("replica", "fsdp", None),
        P("fsdp", None),
        P("fsdp", None),
        P(),
    )
    return jax.shard_map(
        functools.partial(body, mesh.shape["fsdp"], mesh.shape["replica"]),
        mesh=mesh,
        in_specs=placed,
        out_specs=(P("replica", "fsdp", None), P("replica", None)),
        check_vma=False,
    )
```

```python
import functools

import jax
import jax.numpy as jnp
from jax import lax
from jax.experimental import pallas as pl
from jax.experimental.pallas import tpu as pltpu
from jax.sharding import PartitionSpec as P

DOCS = 8
NORM_EPS = 1e-05
ADAM_EPS = 1e-08
INNER_RATE = 0.1
DECAY_RATE = 0.1
BETA_FIRST = 0.9
BETA_SECOND = 0.95
OUTER_RATE = 0.7
NESTEROV = 0.9
MIXING = 0.5
LANES = 128
MESH = pl.DeviceIdType.MESH
F32 = jnp.float32
BF16 = jnp.bfloat16


def adam_update(master, first, second, gradient):
    first = BETA_FIRST * first + (1.0 - BETA_FIRST) * gradient
    second = BETA_SECOND * second + (1.0 - BETA_SECOND) * gradient * gradient
    master = master - INNER_RATE * (first / (jnp.sqrt(second) + ADAM_EPS) + DECAY_RATE * master)
    return (master, first, second)


def partners(me, n):
    if n == 4:
        return [lax.rem(me + 2, 4), 3 - me, me + 1 - 2 * lax.rem(me, 2)]
    return [lax.rem(me + k, n) for k in range(1, n)]


def window_kernel(
    n, replicas, dims,
    hidden, targets_in, ids_in, weights, adam_m, adam_v, anchor, momentum, fragment,
    master_out, first_out, second_out, turned_out, grads_out, loss_out,
    cols, hid, targets, doc_ids, w_ref, m_ref, v_ref, current, master, first, second, turned,
    partial, part_send, part_recv, grads, counts, losses,
    frag_cols, frag_recv, frag_all, anchor_ref, moment_ref, row_scale, token_weight,
    local_sem, out_sem, a2a_send, a2a_recv, count_send, count_recv,
    frag_send, frag_got, all_send, all_got, part_send_sem, part_recv_sem,
    grad_send, grad_recv, loss_send, loss_recv,
):
    steps, tokens, rows, width, model, fw = dims
    own = rows // replicas
    scale = model ** (-0.5)
    rep = lax.axis_index("replica")
    me = lax.axis_index("fsdp")
    others = partners(me, n)
    peers = [lax.rem(rep + k, replicas) for k in range(1, replicas)]

    def block(index, size):
        return pl.ds(pl.multiple_of(index * size, size), size)

    my_tokens = block(me, tokens)
    my_frag = block(rep, own)

    local = [
        pltpu.make_async_copy(weights.at[0], w_ref, local_sem.at[0]),
        pltpu.make_async_copy(hidden.at[0], hid, local_sem.at[1]),
        pltpu.make_async_copy(anchor.at[my_frag, :], anchor_ref, local_sem.at[2]),
        pltpu.make_async_copy(momentum.at[my_frag, :], moment_ref, local_sem.at[3]),
        pltpu.make_async_copy(adam_m.at[0], m_ref, local_sem.at[4]),
        pltpu.make_async_copy(adam_v.at[0], v_ref, local_sem.at[5]),
    ]
    for s in range(steps):
        local.append(pltpu.make_async_copy(
            hidden.at[0, s, :, block(me, rows)], cols.at[s, my_tokens, :], local_sem.at[6 + s]))
    local.append(pltpu.make_async_copy(targets_in, targets, local_sem.at[6 + steps]))
    local.append(pltpu.make_async_copy(ids_in, doc_ids, local_sem.at[7 + steps]))
    for copy in local:
        copy.start()

    barrier = pltpu.get_barrier_semaphore()
    for j in others:
        pl.semaphore_signal(barrier, inc=1, device_id=(rep, j), device_id_type=MESH)
    for i in peers:
        pl.semaphore_signal(barrier, inc=1, device_id=(i, me), device_id_type=MESH)
    pl.semaphore_wait(barrier, n + replicas - 2)

    def a2a(s, j):
        return pltpu.make_async_remote_copy(
            src_ref=hidden.at[0, s, :, block(j, rows)], dst_ref=cols.at[s, my_tokens, :],
            send_sem=a2a_send.at[s, j], recv_sem=a2a_recv.at[s, me],
            device_id=(rep, j), device_id_type=MESH)

    def a2a_arrived(s, j):
        pltpu.make_async_remote_copy(
            src_ref=hidden.at[0, s, :, block(j, rows)], dst_ref=cols.at[s, block(j, tokens), :],
            send_sem=a2a_send.at[s, j], recv_sem=a2a_recv.at[s, j],
            device_id=(rep, j), device_id_type=MESH).wait_recv()

    for j in others:
        a2a(0, j).start()

    local[7 + steps].wait()
    lane = lax.broadcasted_iota(jnp.int32, (tokens, LANES), 1).astype(F32)
    eye = (lax.broadcasted_iota(jnp.int32, (tokens, tokens), 0)
           == lax.broadcasted_iota(jnp.int32, (tokens, tokens), 1))
    onehots = []
    row8 = lax.broadcasted_iota(jnp.int32, (8, LANES), 0)
    tally = jnp.zeros((8, LANES), F32)
    for s in range(steps):
        ids = jnp.broadcast_to(doc_ids[0, s:s + 1, :].astype(F32), (tokens, tokens))
        ids = jnp.sum(jnp.where(eye, ids, 0.0), axis=1, keepdims=True)
        onehot = (ids == lane).astype(F32)
        onehots.append(onehot)
        tally = tally + jnp.where(row8 == s, jnp.sum(onehot, axis=0, keepdims=True), 0.0)
    counts[me] = tally

    def to_all(buf, send, recv, j):
        return pltpu.make_async_remote_copy(
            src_ref=buf.at[me], dst_ref=buf.at[me], send_sem=send.at[j], recv_sem=recv.at[me],
            device_id=(rep, j), device_id_type=MESH)

    def from_all(buf, send, recv, j):
        pltpu.make_async_remote_copy(
            src_ref=buf.at[j], dst_ref=buf.at[j], send_sem=send.at[j], recv_sem=recv.at[j],
            device_id=(rep, j), device_id_type=MESH).wait_recv()

    for j in others:
        to_all(counts, count_send, count_recv, j).start()

    local[0].wait()
    picked = fragment[0]
    for k in range(width // fw):
        piece = w_ref[:, k * fw:(k + 1) * fw]
        if k == 0:
            frag_cols[...] = piece
        else:
            frag_cols[...] = jnp.where(picked == k, piece, frag_cols[...])

    def frag_copy(i):
        return pltpu.make_async_remote_copy(
            src_ref=frag_cols.at[block(i, own), :], dst_ref=frag_recv.at[rep],
            send_sem=frag_send.at[i], recv_sem=frag_got.at[rep],
            device_id=(i, me), device_id_type=MESH)

    for i in peers:
        frag_copy(i).start()
    frag_recv[rep] = frag_cols[my_frag, :]

    local[1].wait()
    wide = 4 * LANES
    for s in range(steps):
        def add_squares(c, acc, s=s):
            x = hid[s, :, block(c, wide)].astype(F32)
            return acc + x * x
        acc = lax.fori_loop(0, model // wide, add_squares, jnp.zeros((tokens, wide), F32))
        power = jnp.sum(acc, axis=1, keepdims=True) / model
        row_scale[s] = jnp.broadcast_to(lax.rsqrt(power + NORM_EPS), (tokens, LANES))

    for j in others:
        from_all(counts, count_send, count_recv, j)
    total = counts[0]
    for j in range(1, n):
        total = total + counts[j]
    inverse = jnp.where(total > 0.0, 1.0 / (DOCS * jnp.maximum(total, 1.0)), 0.0)
    for s in range(steps):
        weight = jnp.sum(onehots[s] * inverse[s:s + 1, :], axis=1, keepdims=True)
        token_weight[s] = jnp.broadcast_to(weight, (tokens, LANES))

    for i in peers:
        pltpu.make_async_remote_copy(
            src_ref=frag_recv.at[i], dst_ref=frag_recv.at[i], send_sem=frag_send.at[i],
            recv_sem=frag_got.at[i], device_id=(i, me), device_id_type=MESH).wait_recv()
    local[2].wait()
    local[3].wait()
    base = anchor_ref[...].astype(F32)
    delta = base - frag_recv[0].astype(F32)
    for i in range(1, replicas):
        delta = delta + (base - frag_recv[i].astype(F32))
    mean_delta = delta / replicas
    new_moment = NESTEROV * moment_ref[...].astype(F32) + mean_delta
    frag_all[my_frag, :] = base - OUTER_RATE * (mean_delta + NESTEROV * new_moment)

    def all_copy(i):
        return pltpu.make_async_remote_copy(
            src_ref=frag_all.at[my_frag, :], dst_ref=frag_all.at[my_frag, :],
            send_sem=all_send.at[i], recv_sem=all_got.at[rep],
            device_id=(i, me), device_id_type=MESH)

    for i in peers:
        all_copy(i).start()

    local[6 + steps].wait()

    for j in others:
        a2a(0, j).wait_send()
        a2a(1, j).start()

    def part_copy(s, j):
        return pltpu.make_async_remote_copy(
            src_ref=part_send.at[s, block(j, tokens), :], dst_ref=part_recv.at[s, me],
            send_sem=part_send_sem.at[s, j], recv_sem=part_recv_sem.at[s, me],
            device_id=(rep, j), device_id_type=MESH)

    def grad_copy(s, j):
        return pltpu.make_async_remote_copy(
            src_ref=grads.at[s, my_tokens, :], dst_ref=grads.at[s, my_tokens, :],
            send_sem=grad_send.at[s, j], recv_sem=grad_recv.at[s, me],
            device_id=(rep, j), device_id_type=MESH)

    tile = 256

    def project_and_share(s, held):
        for j in others:
            a2a_arrived(s, j)
        local[6 + s].wait()

        @pl.loop(0, width // tile)
        def _(c):
            at = block(c, tile)
            out = jnp.dot(cols[s], held[:, at], preferred_element_type=F32)
            partial[:, at] = out
            part_send[s, :, at] = out.astype(BF16)

        for j in others:
            part_copy(s, j).start()

        @pl.loop(0, rows // tile)
        def _(c):
            at = block(c, tile)
            turned[s, at, :] = cols[s, :, at].T

        values = partial[my_tokens, :]
        for j in others:
            pltpu.make_async_remote_copy(
                src_ref=part_recv.at[s, j], dst_ref=part_recv.at[s, j],
                send_sem=part_send_sem.at[s, j], recv_sem=part_recv_sem.at[s, j],
                device_id=(rep, j), device_id_type=MESH).wait_recv()
            values = values + part_recv[s, j].astype(F32)
        gain = row_scale[s][:, :1]
        weight = token_weight[s][:, :1]
        error = values * (gain * scale) - targets[0, s].astype(F32)
        grads[s, my_tokens, :] = ((weight * gain / width) * error).astype(BF16)
        for j in others:
            grad_copy(s, j).start()
        loss = jnp.sum(weight * 0.5 * jnp.mean(error * error, axis=-1, keepdims=True))
        loss = jnp.where(row8 == s, loss, 0.0)
        if s == 0:
            losses[me] = loss
        else:
            losses[me] = losses[me] + loss
        if s == steps - 1:
            for j in others:
                to_all(losses, loss_send, loss_recv, j).start()
        for j in others:
            pltpu.make_async_remote_copy(
                src_ref=grads.at[s, block(j, tokens), :], dst_ref=grads.at[s, block(j, tokens), :],
                send_sem=grad_send.at[s, j], recv_sem=grad_recv.at[s, j],
                device_id=(rep, j), device_id_type=MESH).wait_recv()

    project_and_share(0, w_ref)
    local[4].wait()
    local[5].wait()
    rt = 128

    for i in peers:
        at = block(i, own)
        pltpu.make_async_remote_copy(
            src_ref=frag_all.at[at, :], dst_ref=frag_all.at[at, :], send_sem=all_send.at[i],
            recv_sem=all_got.at[i], device_id=(i, me), device_id_type=MESH).wait_recv()

    @pl.loop(0, rows // rt)
    def _(c):
        at = block(c, rt)
        gradient = jnp.dot(turned[0, at, :], grads[0], preferred_element_type=F32) * scale
        new_master, new_first, new_second = adam_update(
            w_ref[at, :].astype(F32), m_ref[at, :].astype(F32), v_ref[at, :].astype(F32), gradient)
        current[at, :] = new_master.astype(BF16)
        first[at, :] = (INNER_RATE * BETA_FIRST) * new_first
        second[at, :] = BETA_SECOND * new_second
        kept = (1.0 - INNER_RATE * DECAY_RATE) * new_master
        mixed = (1.0 - MIXING) * frag_all[at, :]
        for k in range(width // fw):
            piece = kept[:, k * fw:(k + 1) * fw]
            master[at, k * fw:(k + 1) * fw] = jnp.where(picked == k, MIXING * piece + mixed, piece)

    outs = [
        pltpu.make_async_copy(master, master_out, out_sem.at[0]),
        pltpu.make_async_copy(first, first_out, out_sem.at[1]),
        pltpu.make_async_copy(second, second_out, out_sem.at[2]),
    ]
    for copy in outs:
        copy.start()

    project_and_share(1, current)
    outs.append(pltpu.make_async_copy(turned.at[1], turned_out, out_sem.at[3]))
    outs.append(pltpu.make_async_copy(grads.at[1], grads_out, out_sem.at[4]))
    outs[-2].start()
    outs[-1].start()
    for j in others:
        from_all(losses, loss_send, loss_recv, j)
    loss = losses[0]
    for j in range(1, n):
        loss = loss + losses[j]
    loss_out[...] = loss

    for j in others:
        a2a(1, j).wait_send()
        to_all(counts, count_send, count_recv, j).wait_send()
        to_all(losses, loss_send, loss_recv, j).wait_send()
        for s in range(steps):
            part_copy(s, j).wait_send()
            grad_copy(s, j).wait_send()
    for i in peers:
        frag_copy(i).wait_send()
        all_copy(i).wait_send()
    for copy in outs:
        copy.wait()


def finish_kernel(scale, fw, fragment, kept, first, second, turned, grads, loss, out, loss_out):
    raw = jnp.dot(turned[...], grads[...], preferred_element_type=F32)
    moved = first[...] + (INNER_RATE * (1.0 - BETA_FIRST) * scale) * raw
    power = second[...] + ((1.0 - BETA_SECOND) * scale * scale) * (raw * raw)
    step = moved / (power * lax.rsqrt(power) + ADAM_EPS)
    width = out.shape[2]
    column = lax.broadcasted_iota(jnp.int32, (1, width), 1) // fw
    share = jnp.where(column == fragment[0], MIXING, 1.0)
    out[0] = kept[...] - share * step
    steps = loss_out.shape[1]
    across = lax.broadcasted_iota(jnp.int32, (1, steps), 1)
    line = jnp.zeros((1, steps), F32)
    for s in range(steps):
        line = jnp.where(across == s, loss[s:s + 1, :steps], line)
    loss_out[...] = line


def body(n, replicas, hidden, targets, doc_ids, weights, adam_m, adam_v, anchor, momentum, fragment):
    steps, tokens, model = hidden.shape[1:]
    rows, width = weights.shape[1:]
    fw = anchor.shape[1]
    own = rows // replicas
    everyone = n * tokens
    dims = (steps, tokens, rows, width, model, fw)
    any_spec = pl.BlockSpec(memory_space=pltpu.HBM)
    vmem = pl.BlockSpec(memory_space=pltpu.VMEM)
    smem = pl.BlockSpec(memory_space=pltpu.SMEM)
    dma = pltpu.SemaphoreType.DMA
    shape = jax.ShapeDtypeStruct
    master, first, second, turned, grads, loss = pl.pallas_call(
        functools.partial(window_kernel, n, replicas, dims),
        out_shape=[
            shape((rows, width), F32), shape((rows, width), F32), shape((rows, width), F32),
            shape((rows, everyone), BF16), shape((everyone, width), BF16),
            shape((8, LANES), F32),
        ],
        in_specs=[any_spec, any_spec, any_spec, any_spec, any_spec, any_spec, any_spec, any_spec, smem],
        out_specs=[any_spec] * 5 + [vmem],
        scratch_shapes=[
            pltpu.VMEM((steps, everyone, rows), BF16),
            pltpu.VMEM((steps, tokens, model), BF16),
            pltpu.VMEM((1, steps, tokens, width), BF16),
            pltpu.VMEM((1, steps, tokens), jnp.int32),
            pltpu.VMEM((rows, width), BF16),
            pltpu.VMEM((rows, width), BF16),
            pltpu.VMEM((rows, width), BF16),
            pltpu.VMEM((rows, width), BF16),
            pltpu.VMEM((rows, width), F32),
            pltpu.VMEM((rows, width), F32),
            pltpu.VMEM((rows, width), F32),
            pltpu.VMEM((steps, rows, everyone), BF16),
            pltpu.VMEM((everyone, width), F32),
            pltpu.VMEM((steps, everyone, width), BF16),
            pltpu.VMEM((steps, n, tokens, width), BF16),
            pltpu.VMEM((steps, everyone, width), BF16),
            pltpu.VMEM((n, 8, LANES), F32),
            pltpu.VMEM((n, 8, LANES), F32),
            pltpu.VMEM((rows, fw), BF16),
            pltpu.VMEM((replicas, own, fw), BF16),
            pltpu.VMEM((rows, fw), F32),
            pltpu.VMEM((own, fw), BF16),
            pltpu.VMEM((own, fw), BF16),
            pltpu.VMEM((steps, tokens, LANES), F32),
            pltpu.VMEM((steps, tokens, LANES), F32),
            dma((8 + steps,)), dma((5,)),
            dma((steps, n)), dma((steps, n)), dma((n,)), dma((n,)),
            dma((replicas,)), dma((replicas,)), dma((replicas,)), dma((replicas,)),
            dma((steps, n)), dma((steps, n)),
            dma((steps, n)), dma((steps, n)), dma((n,)), dma((n,)),
        ],
        compiler_params=pltpu.CompilerParams(
            collective_id=0, has_side_effects=True, vmem_limit_bytes=60 * 1024 * 1024),
        name="window",
    )(hidden, targets, doc_ids, weights, adam_m, adam_v, anchor, momentum, fragment)

    rt = min(256, rows)
    whole = lambda shape: pl.BlockSpec(shape, lambda i: (0, 0))
    piece = lambda cols: pl.BlockSpec((rt, cols), lambda i: (i, 0))
    return pl.pallas_call(
        functools.partial(finish_kernel, model ** (-0.5), fw),
        grid=(rows // rt,),
        out_shape=[shape((1, rows, width), F32), shape((1, steps), F32)],
        in_specs=[smem, piece(width), piece(width), piece(width), piece(everyone),
                  whole((everyone, width)), whole((8, LANES))],
        out_specs=[pl.BlockSpec((1, rt, width), lambda i: (0, i, 0)), whole((1, steps))],
        compiler_params=pltpu.CompilerParams(vmem_limit_bytes=60 * 1024 * 1024),
        name="finish",
    )(fragment, master, first, second, turned, grads, loss)


def solution(mesh):
    placed = (
        P("replica", None, "fsdp", None),
        P("replica", None, "fsdp", None),
        P("replica", None, "fsdp"),
        P("replica", "fsdp", None),
        P("replica", "fsdp", None),
        P("replica", "fsdp", None),
        P("fsdp", None),
        P("fsdp", None),
        P(),
    )
    return jax.shard_map(
        functools.partial(body, mesh.shape["fsdp"], mesh.shape["replica"]),
        mesh=mesh,
        in_specs=placed,
        out_specs=(P("replica", "fsdp", None), P("replica", None)),
        check_vma=False,
    )
```

```python
import functools

import jax
import jax.numpy as jnp
from jax import lax
from jax.experimental import pallas as pl
from jax.experimental.pallas import tpu as pltpu
from jax.sharding import PartitionSpec as P

DOCS = 8
NORM_EPS = 1e-05
ADAM_EPS = 1e-08
INNER_RATE = 0.1
DECAY_RATE = 0.1
BETA_FIRST = 0.9
BETA_SECOND = 0.95
OUTER_RATE = 0.7
NESTEROV = 0.9
MIXING = 0.5
LANES = 128
MESH = pl.DeviceIdType.MESH
F32 = jnp.float32
BF16 = jnp.bfloat16


def adam_update(master, first, second, gradient):
    first = BETA_FIRST * first + (1.0 - BETA_FIRST) * gradient
    second = BETA_SECOND * second + (1.0 - BETA_SECOND) * gradient * gradient
    master = master - INNER_RATE * (first / (jnp.sqrt(second) + ADAM_EPS) + DECAY_RATE * master)
    return (master, first, second)


def partners(me, n):
    if n == 4:
        return [lax.rem(me + 2, 4), 3 - me, me + 1 - 2 * lax.rem(me, 2)]
    return [lax.rem(me + k, n) for k in range(1, n)]


def window_kernel(
    n, replicas, dims,
    hidden, targets_in, ids_in, weights, adam_m, adam_v, anchor, momentum, fragment,
    master, first, second, turned, grads, loss_out,
    cols, hid, targets, doc_ids, w_ref, m_ref, v_ref, current,
    partial, part_send, part_recv, counts, losses,
    frag_cols, frag_recv, frag_all, anchor_ref, moment_ref, row_scale, token_weight,
    local_sem, a2a_send, a2a_recv, count_send, count_recv,
    frag_send, frag_got, all_send, all_got, part_send_sem, part_recv_sem,
    grad_send, grad_recv, loss_send, loss_recv,
):
    steps, tokens, rows, width, model, fw = dims
    own = rows // replicas
    scale = model ** (-0.5)
    rep = lax.axis_index("replica")
    me = lax.axis_index("fsdp")
    others = partners(me, n)
    peers = [lax.rem(rep + k, replicas) for k in range(1, replicas)]

    def block(index, size):
        return pl.ds(pl.multiple_of(index * size, size), size)

    my_tokens = block(me, tokens)
    my_frag = block(rep, own)

    local = [
        pltpu.make_async_copy(weights.at[0], w_ref, local_sem.at[0]),
        pltpu.make_async_copy(hidden.at[0], hid, local_sem.at[1]),
        pltpu.make_async_copy(anchor.at[my_frag, :], anchor_ref, local_sem.at[2]),
        pltpu.make_async_copy(momentum.at[my_frag, :], moment_ref, local_sem.at[3]),
        pltpu.make_async_copy(adam_m.at[0], m_ref, local_sem.at[4]),
        pltpu.make_async_copy(adam_v.at[0], v_ref, local_sem.at[5]),
    ]
    for s in range(steps):
        local.append(pltpu.make_async_copy(
            hidden.at[0, s, :, block(me, rows)], cols.at[s, my_tokens, :], local_sem.at[6 + s]))
    local.append(pltpu.make_async_copy(targets_in, targets, local_sem.at[6 + steps]))
    local.append(pltpu.make_async_copy(ids_in, doc_ids, local_sem.at[7 + steps]))
    for copy in local:
        copy.start()

    barrier = pltpu.get_barrier_semaphore()
    for j in others:
        pl.semaphore_signal(barrier, inc=1, device_id=(rep, j), device_id_type=MESH)
    for i in peers:
        pl.semaphore_signal(barrier, inc=1, device_id=(i, me), device_id_type=MESH)
    pl.semaphore_wait(barrier, n + replicas - 2)

    def a2a(s, j):
        return pltpu.make_async_remote_copy(
            src_ref=hidden.at[0, s, :, block(j, rows)], dst_ref=cols.at[s, my_tokens, :],
            send_sem=a2a_send.at[s, j], recv_sem=a2a_recv.at[s, me],
            device_id=(rep, j), device_id_type=MESH)

    def a2a_arrived(s, j):
        pltpu.make_async_remote_copy(
            src_ref=hidden.at[0, s, :, block(j, rows)], dst_ref=cols.at[s, block(j, tokens), :],
            send_sem=a2a_send.at[s, j], recv_sem=a2a_recv.at[s, j],
            device_id=(rep, j), device_id_type=MESH).wait_recv()

    for j in others:
        a2a(0, j).start()

    local[7 + steps].wait()
    lane = lax.broadcasted_iota(jnp.int32, (tokens, LANES), 1).astype(F32)
    eye = (lax.broadcasted_iota(jnp.int32, (tokens, tokens), 0)
           == lax.broadcasted_iota(jnp.int32, (tokens, tokens), 1))
    onehots = []
    row8 = lax.broadcasted_iota(jnp.int32, (8, LANES), 0)
    tally = jnp.zeros((8, LANES), F32)
    for s in range(steps):
        ids = jnp.broadcast_to(doc_ids[0, s:s + 1, :].astype(F32), (tokens, tokens))
        ids = jnp.sum(jnp.where(eye, ids, 0.0), axis=1, keepdims=True)
        onehot = (ids == lane).astype(F32)
        onehots.append(onehot)
        tally = tally + jnp.where(row8 == s, jnp.sum(onehot, axis=0, keepdims=True), 0.0)
    counts[me] = tally

    def to_all(buf, send, recv, j):
        return pltpu.make_async_remote_copy(
            src_ref=buf.at[me], dst_ref=buf.at[me], send_sem=send.at[j], recv_sem=recv.at[me],
            device_id=(rep, j), device_id_type=MESH)

    def from_all(buf, send, recv, j):
        pltpu.make_async_remote_copy(
            src_ref=buf.at[j], dst_ref=buf.at[j], send_sem=send.at[j], recv_sem=recv.at[j],
            device_id=(rep, j), device_id_type=MESH).wait_recv()

    for j in others:
        to_all(counts, count_send, count_recv, j).start()

    local[0].wait()
    picked = fragment[0]
    for k in range(width // fw):
        piece = w_ref[:, k * fw:(k + 1) * fw]
        if k == 0:
            frag_cols[...] = piece
        else:
            frag_cols[...] = jnp.where(picked == k, piece, frag_cols[...])

    def frag_copy(i):
        return pltpu.make_async_remote_copy(
            src_ref=frag_cols.at[block(i, own), :], dst_ref=frag_recv.at[rep],
            send_sem=frag_send.at[i], recv_sem=frag_got.at[rep],
            device_id=(i, me), device_id_type=MESH)

    for i in peers:
        frag_copy(i).start()
    frag_recv[rep] = frag_cols[my_frag, :]

    local[1].wait()
    wide = 4 * LANES
    for s in range(steps):
        def add_squares(c, acc, s=s):
            x = hid[s, :, block(c, wide)].astype(F32)
            return acc + x * x
        acc = lax.fori_loop(0, model // wide, add_squares, jnp.zeros((tokens, wide), F32))
        power = jnp.sum(acc, axis=1, keepdims=True) / model
        row_scale[s] = jnp.broadcast_to(lax.rsqrt(power + NORM_EPS), (tokens, LANES))

    for j in others:
        from_all(counts, count_send, count_recv, j)
    total = counts[0]
    for j in range(1, n):
        total = total + counts[j]
    inverse = jnp.where(total > 0.0, 1.0 / (DOCS * jnp.maximum(total, 1.0)), 0.0)
    for s in range(steps):
        weight = jnp.sum(onehots[s] * inverse[s:s + 1, :], axis=1, keepdims=True)
        token_weight[s] = jnp.broadcast_to(weight, (tokens, LANES))

    for i in peers:
        pltpu.make_async_remote_copy(
            src_ref=frag_recv.at[i], dst_ref=frag_recv.at[i], send_sem=frag_send.at[i],
            recv_sem=frag_got.at[i], device_id=(i, me), device_id_type=MESH).wait_recv()
    local[2].wait()
    local[3].wait()
    base = anchor_ref[...].astype(F32)
    delta = base - frag_recv[0].astype(F32)
    for i in range(1, replicas):
        delta = delta + (base - frag_recv[i].astype(F32))
    mean_delta = delta / replicas
    new_moment = NESTEROV * moment_ref[...].astype(F32) + mean_delta
    frag_all[my_frag, :] = base - OUTER_RATE * (mean_delta + NESTEROV * new_moment)

    def all_copy(i):
        return pltpu.make_async_remote_copy(
            src_ref=frag_all.at[my_frag, :], dst_ref=frag_all.at[my_frag, :],
            send_sem=all_send.at[i], recv_sem=all_got.at[rep],
            device_id=(i, me), device_id_type=MESH)

    for i in peers:
        all_copy(i).start()

    local[6 + steps].wait()

    for j in others:
        a2a(0, j).wait_send()
        a2a(1, j).start()

    def part_copy(s, j):
        return pltpu.make_async_remote_copy(
            src_ref=part_send.at[s, block(j, tokens), :], dst_ref=part_recv.at[s, me],
            send_sem=part_send_sem.at[s, j], recv_sem=part_recv_sem.at[s, me],
            device_id=(rep, j), device_id_type=MESH)

    def grad_copy(s, j):
        return pltpu.make_async_remote_copy(
            src_ref=grads.at[s, my_tokens, :], dst_ref=grads.at[s, my_tokens, :],
            send_sem=grad_send.at[s, j], recv_sem=grad_recv.at[s, me],
            device_id=(rep, j), device_id_type=MESH)

    tile = 256

    def project_and_share(s, held):
        for j in others:
            a2a_arrived(s, j)
        local[6 + s].wait()

        @pl.loop(0, width // tile)
        def _(c):
            at = block(c, tile)
            out = jnp.dot(cols[s], held[:, at], preferred_element_type=F32)
            partial[:, at] = out
            part_send[s, :, at] = out.astype(BF16)

        for j in others:
            part_copy(s, j).start()

        @pl.loop(0, rows // tile)
        def _(c):
            at = block(c, tile)
            turned[s, at, :] = cols[s, :, at].T

        values = partial[my_tokens, :]
        for j in others:
            pltpu.make_async_remote_copy(
                src_ref=part_recv.at[s, j], dst_ref=part_recv.at[s, j],
                send_sem=part_send_sem.at[s, j], recv_sem=part_recv_sem.at[s, j],
                device_id=(rep, j), device_id_type=MESH).wait_recv()
            values = values + part_recv[s, j].astype(F32)
        gain = row_scale[s][:, :1]
        weight = token_weight[s][:, :1]
        error = values * (gain * scale) - targets[0, s].astype(F32)
        grads[s, my_tokens, :] = ((weight * gain / width) * error).astype(BF16)
        for j in others:
            grad_copy(s, j).start()
        loss = jnp.sum(weight * 0.5 * jnp.mean(error * error, axis=-1, keepdims=True))
        loss = jnp.where(row8 == s, loss, 0.0)
        if s == 0:
            losses[me] = loss
        else:
            losses[me] = losses[me] + loss
        if s == steps - 1:
            for j in others:
                to_all(losses, loss_send, loss_recv, j).start()
        for j in others:
            pltpu.make_async_remote_copy(
                src_ref=grads.at[s, block(j, tokens), :], dst_ref=grads.at[s, block(j, tokens), :],
                send_sem=grad_send.at[s, j], recv_sem=grad_recv.at[s, j],
                device_id=(rep, j), device_id_type=MESH).wait_recv()

    project_and_share(0, w_ref)
    local[4].wait()
    local[5].wait()
    rt = 128

    for i in peers:
        at = block(i, own)
        pltpu.make_async_remote_copy(
            src_ref=frag_all.at[at, :], dst_ref=frag_all.at[at, :], send_sem=all_send.at[i],
            recv_sem=all_got.at[i], device_id=(i, me), device_id_type=MESH).wait_recv()

    @pl.loop(0, rows // rt)
    def _(c):
        at = block(c, rt)
        gradient = jnp.dot(turned[0, at, :], grads[0], preferred_element_type=F32) * scale
        new_master, new_first, new_second = adam_update(
            w_ref[at, :].astype(F32), m_ref[at, :].astype(F32), v_ref[at, :].astype(F32), gradient)
        current[at, :] = new_master.astype(BF16)
        first[at, :] = (INNER_RATE * BETA_FIRST) * new_first
        second[at, :] = BETA_SECOND * new_second
        kept = (1.0 - INNER_RATE * DECAY_RATE) * new_master
        mixed = (1.0 - MIXING) * frag_all[at, :]
        for k in range(width // fw):
            piece = kept[:, k * fw:(k + 1) * fw]
            master[at, k * fw:(k + 1) * fw] = jnp.where(picked == k, MIXING * piece + mixed, piece)

    project_and_share(1, current)
    for j in others:
        from_all(losses, loss_send, loss_recv, j)
    loss = losses[0]
    for j in range(1, n):
        loss = loss + losses[j]
    loss_out[...] = loss

    for j in others:
        a2a(1, j).wait_send()
        to_all(counts, count_send, count_recv, j).wait_send()
        to_all(losses, loss_send, loss_recv, j).wait_send()
        for s in range(steps):
            part_copy(s, j).wait_send()
            grad_copy(s, j).wait_send()
    for i in peers:
        frag_copy(i).wait_send()
        all_copy(i).wait_send()


def finish_kernel(scale, fw, fragment, kept, first, second, turned, grads, loss, out, loss_out,
                  done, out_sem):
    rows, width = kept.shape
    last = turned.shape[0] - 1
    tiles = out_sem.shape[0]
    rt = rows // tiles
    column = lax.broadcasted_iota(jnp.int32, (1, width), 1) // fw
    share = jnp.where(column == fragment[0], MIXING, 1.0)

    def write(c):
        at = pl.ds(pl.multiple_of(c * rt, rt), rt)
        return pltpu.make_async_copy(done.at[at, :], out.at[0, at, :], out_sem.at[c])

    @pl.loop(0, tiles)
    def _(c):
        at = pl.ds(pl.multiple_of(c * rt, rt), rt)
        raw = jnp.dot(turned[last, at, :], grads[last], preferred_element_type=F32)
        moved = first[at, :] + (INNER_RATE * (1.0 - BETA_FIRST) * scale) * raw
        power = second[at, :] + ((1.0 - BETA_SECOND) * scale * scale) * (raw * raw)
        step = moved / (power * lax.rsqrt(power) + ADAM_EPS)
        done[at, :] = kept[at, :] - share * step
        write(c).start()

    steps = loss_out.shape[1]
    across = lax.broadcasted_iota(jnp.int32, (1, steps), 1)
    line = jnp.zeros((1, steps), F32)
    for s in range(steps):
        line = jnp.where(across == s, loss[s:s + 1, :steps], line)
    loss_out[...] = line

    @pl.loop(0, tiles)
    def _(c):
        write(c).wait()


def body(n, replicas, hidden, targets, doc_ids, weights, adam_m, adam_v, anchor, momentum, fragment):
    steps, tokens, model = hidden.shape[1:]
    rows, width = weights.shape[1:]
    fw = anchor.shape[1]
    own = rows // replicas
    everyone = n * tokens
    dims = (steps, tokens, rows, width, model, fw)
    any_spec = pl.BlockSpec(memory_space=pltpu.HBM)
    vmem = pl.BlockSpec(memory_space=pltpu.VMEM)
    smem = pl.BlockSpec(memory_space=pltpu.SMEM)
    dma = pltpu.SemaphoreType.DMA
    shape = jax.ShapeDtypeStruct
    outer = [pltpu.with_memory_space_constraint(x, pltpu.HBM) for x in (
        hidden, targets, doc_ids, weights, adam_m, adam_v, anchor, momentum)]
    master, first, second, turned, grads, loss = pl.pallas_call(
        functools.partial(window_kernel, n, replicas, dims),
        out_shape=[
            pltpu.VMEM((rows, width), F32), pltpu.VMEM((rows, width), F32),
            pltpu.VMEM((rows, width), F32), pltpu.VMEM((steps, rows, everyone), BF16),
            pltpu.VMEM((steps, everyone, width), BF16), pltpu.VMEM((8, LANES), F32),
        ],
        in_specs=[any_spec] * 8 + [smem],
        out_specs=[vmem] * 6,
        scratch_shapes=[
            pltpu.VMEM((steps, everyone, rows), BF16),
            pltpu.VMEM((steps, tokens, model), BF16),
            pltpu.VMEM((1, steps, tokens, width), BF16),
            pltpu.VMEM((1, steps, tokens), jnp.int32),
            pltpu.VMEM((rows, width), BF16),
            pltpu.VMEM((rows, width), BF16),
            pltpu.VMEM((rows, width), BF16),
            pltpu.VMEM((rows, width), BF16),
            pltpu.VMEM((everyone, width), F32),
            pltpu.VMEM((steps, everyone, width), BF16),
            pltpu.VMEM((steps, n, tokens, width), BF16),
            pltpu.VMEM((n, 8, LANES), F32),
            pltpu.VMEM((n, 8, LANES), F32),
            pltpu.VMEM((rows, fw), BF16),
            pltpu.VMEM((replicas, own, fw), BF16),
            pltpu.VMEM((rows, fw), F32),
            pltpu.VMEM((own, fw), BF16),
            pltpu.VMEM((own, fw), BF16),
            pltpu.VMEM((steps, tokens, LANES), F32),
            pltpu.VMEM((steps, tokens, LANES), F32),
            dma((8 + steps,)),
            dma((steps, n)), dma((steps, n)), dma((n,)), dma((n,)),
            dma((replicas,)), dma((replicas,)), dma((replicas,)), dma((replicas,)),
            dma((steps, n)), dma((steps, n)),
            dma((steps, n)), dma((steps, n)), dma((n,)), dma((n,)),
        ],
        compiler_params=pltpu.CompilerParams(
            collective_id=0, has_side_effects=True, vmem_limit_bytes=28 * 1024 * 1024),
        name="window",
    )(*outer, fragment)

    inner = [pltpu.with_memory_space_constraint(x, pltpu.VMEM)
             for x in (master, first, second, turned, grads, loss)]
    return pl.pallas_call(
        functools.partial(finish_kernel, model ** (-0.5), fw),
        out_shape=[shape((1, rows, width), F32), shape((1, steps), F32)],
        in_specs=[smem] + [vmem] * 6,
        out_specs=[any_spec, vmem],
        scratch_shapes=[pltpu.VMEM((rows, width), F32), dma((8,))],
        compiler_params=pltpu.CompilerParams(vmem_limit_bytes=16 * 1024 * 1024),
        name="finish",
    )(fragment, *inner)


def solution(mesh):
    placed = (
        P("replica", None, "fsdp", None),
        P("replica", None, "fsdp", None),
        P("replica", None, "fsdp"),
        P("replica", "fsdp", None),
        P("replica", "fsdp", None),
        P("replica", "fsdp", None),
        P("fsdp", None),
        P("fsdp", None),
        P(),
    )
    return jax.shard_map(
        functools.partial(body, mesh.shape["fsdp"], mesh.shape["replica"]),
        mesh=mesh,
        in_specs=placed,
        out_specs=(P("replica", "fsdp", None), P("replica", None)),
        check_vma=False,
    )
```

```python
import functools

import jax
import jax.numpy as jnp
from jax import lax
from jax.experimental import pallas as pl
from jax.experimental.pallas import tpu as pltpu
from jax.sharding import PartitionSpec as P

DOCS = 8
NORM_EPS = 1e-05
ADAM_EPS = 1e-08
INNER_RATE = 0.1
DECAY_RATE = 0.1
BETA_FIRST = 0.9
BETA_SECOND = 0.95
OUTER_RATE = 0.7
NESTEROV = 0.9
MIXING = 0.5
LANES = 128
MESH = pl.DeviceIdType.MESH
F32 = jnp.float32
BF16 = jnp.bfloat16


def adam_update(master, first, second, gradient):
    first = BETA_FIRST * first + (1.0 - BETA_FIRST) * gradient
    second = BETA_SECOND * second + (1.0 - BETA_SECOND) * gradient * gradient
    master = master - INNER_RATE * (first / (jnp.sqrt(second) + ADAM_EPS) + DECAY_RATE * master)
    return (master, first, second)


def partners(me, n):
    if n == 4:
        return [lax.rem(me + 2, 4), 3 - me, me + 1 - 2 * lax.rem(me, 2)]
    return [lax.rem(me + k, n) for k in range(1, n)]


def window_kernel(
    n, replicas, dims,
    hidden, targets_in, ids_in, weights, adam_m, adam_v, anchor, momentum, fragment,
    master, first, second, turned, grads, loss_out,
    cols, hid, targets, doc_ids, w_ref, m_ref, v_ref, current,
    partial, part_send, part_recv, counts, losses,
    frag_cols, frag_recv, frag_all, anchor_ref, moment_ref, row_scale, token_weight,
    coef_mine, coef_got, coef_across, coef_sem,
    local_sem, a2a_send, a2a_recv, count_send, count_recv,
    frag_send, frag_got, all_send, all_got, part_send_sem, part_recv_sem,
    grad_send, grad_recv, loss_send, loss_recv,
):
    steps, tokens, rows, width, model, fw = dims
    paired = n == 4 and tokens <= LANES
    units = cols.shape[0]
    parts = units // steps
    few = tokens // parts
    together = n * few
    own = rows // replicas
    scale = model ** (-0.5)
    rep = lax.axis_index("replica")
    me = lax.axis_index("fsdp")
    others = partners(me, n)
    peers = [lax.rem(rep + k, replicas) for k in range(1, replicas)]

    def block(index, size):
        return pl.ds(pl.multiple_of(index * size, size), size)

    def slot(j):
        return 2 * lax.rem(j, 2) + j // 2 if paired else j

    my_tokens = block(slot(me), few)
    my_frag = block(rep, own)

    local = [
        pltpu.make_async_copy(weights.at[0], w_ref, local_sem.at[0]),
        pltpu.make_async_copy(hidden.at[0], hid, local_sem.at[1]),
        pltpu.make_async_copy(anchor.at[my_frag, :], anchor_ref, local_sem.at[2]),
        pltpu.make_async_copy(momentum.at[my_frag, :], moment_ref, local_sem.at[3]),
        pltpu.make_async_copy(adam_m.at[0], m_ref, local_sem.at[4]),
        pltpu.make_async_copy(adam_v.at[0], v_ref, local_sem.at[5]),
    ]

    def held_tokens(u, j):
        return hidden.at[0, u // parts, u % parts * few:(u % parts + 1) * few, block(j, rows)]

    for u in range(units):
        local.append(pltpu.make_async_copy(
            held_tokens(u, me), cols.at[u, my_tokens, :], local_sem.at[6 + u]))
    local.append(pltpu.make_async_copy(targets_in, targets, local_sem.at[6 + units]))
    local.append(pltpu.make_async_copy(ids_in, doc_ids, local_sem.at[7 + units]))
    for copy in local:
        copy.start()

    barrier = pltpu.get_barrier_semaphore()
    for j in others:
        pl.semaphore_signal(barrier, inc=1, device_id=(rep, j), device_id_type=MESH)
    for i in peers:
        pl.semaphore_signal(barrier, inc=1, device_id=(i, me), device_id_type=MESH)
    pl.semaphore_wait(barrier, n + replicas - 2)

    def a2a(u, j):
        return pltpu.make_async_remote_copy(
            src_ref=held_tokens(u, j), dst_ref=cols.at[u, my_tokens, :],
            send_sem=a2a_send.at[u, j], recv_sem=a2a_recv.at[u, me],
            device_id=(rep, j), device_id_type=MESH)

    def a2a_arrived(u, j):
        pltpu.make_async_remote_copy(
            src_ref=held_tokens(u, j), dst_ref=cols.at[u, block(slot(j), few), :],
            send_sem=a2a_send.at[u, j], recv_sem=a2a_recv.at[u, j],
            device_id=(rep, j), device_id_type=MESH).wait_recv()

    for u in range(min(2, units)):
        for j in others:
            a2a(u, j).start()

    local[7 + units].wait()
    lane = lax.broadcasted_iota(jnp.int32, (tokens, LANES), 1).astype(F32)
    eye = (lax.broadcasted_iota(jnp.int32, (tokens, tokens), 0)
           == lax.broadcasted_iota(jnp.int32, (tokens, tokens), 1))
    wide_eye = (lax.broadcasted_iota(jnp.int32, (tokens, LANES), 0)
                == lax.broadcasted_iota(jnp.int32, (tokens, LANES), 1))
    onehots = []
    row8 = lax.broadcasted_iota(jnp.int32, (8, LANES), 0)
    tally = jnp.zeros((8, LANES), F32)
    for s in range(steps):
        ids = jnp.broadcast_to(doc_ids[0, s:s + 1, :].astype(F32), (tokens, tokens))
        ids = jnp.sum(jnp.where(eye, ids, 0.0), axis=1, keepdims=True)
        onehot = (ids == lane).astype(F32)
        onehots.append(onehot)
        tally = tally + jnp.where(row8 == s, jnp.sum(onehot, axis=0, keepdims=True), 0.0)
    counts[me] = tally

    def to_all(buf, send, recv, j):
        return pltpu.make_async_remote_copy(
            src_ref=buf.at[me], dst_ref=buf.at[me], send_sem=send.at[j], recv_sem=recv.at[me],
            device_id=(rep, j), device_id_type=MESH)

    def from_all(buf, send, recv, j):
        pltpu.make_async_remote_copy(
            src_ref=buf.at[j], dst_ref=buf.at[j], send_sem=send.at[j], recv_sem=recv.at[j],
            device_id=(rep, j), device_id_type=MESH).wait_recv()

    for j in others:
        to_all(counts, count_send, count_recv, j).start()

    local[0].wait()
    picked = fragment[0]
    for k in range(width // fw):
        piece = w_ref[:, k * fw:(k + 1) * fw]
        if k == 0:
            frag_cols[...] = piece
        else:
            frag_cols[...] = jnp.where(picked == k, piece, frag_cols[...])

    def frag_copy(i):
        return pltpu.make_async_remote_copy(
            src_ref=frag_cols.at[block(i, own), :], dst_ref=frag_recv.at[rep],
            send_sem=frag_send.at[i], recv_sem=frag_got.at[rep],
            device_id=(i, me), device_id_type=MESH)

    for i in peers:
        frag_copy(i).start()
    frag_recv[rep] = frag_cols[my_frag, :]

    local[1].wait()
    wide = 4 * LANES
    for s in range(steps):
        def add_squares(c, acc, s=s):
            x = hid[s, :, block(c, wide)].astype(F32)
            return acc + x * x
        acc = lax.fori_loop(0, model // wide, add_squares, jnp.zeros((tokens, wide), F32))
        power = jnp.sum(acc, axis=1, keepdims=True) / model
        row_scale[s] = jnp.broadcast_to(lax.rsqrt(power + NORM_EPS), (tokens, LANES))

    for j in others:
        from_all(counts, count_send, count_recv, j)
    total = counts[0]
    for j in range(1, n):
        total = total + counts[j]
    inverse = jnp.where(total > 0.0, 1.0 / (DOCS * jnp.maximum(total, 1.0)), 0.0)
    for s in range(steps):
        weight = jnp.sum(onehots[s] * inverse[s:s + 1, :], axis=1, keepdims=True)
        token_weight[s] = jnp.broadcast_to(weight, (tokens, LANES))

    def across():
        return pltpu.make_async_remote_copy(
            src_ref=coef_mine, dst_ref=coef_got, send_sem=coef_sem.at[0], recv_sem=coef_sem.at[1],
            device_id=(rep, lax.rem(me + 2, n)), device_id_type=MESH)

    if paired:
        lines = jnp.zeros((8, LANES), F32)
        for s in range(steps):
            coef = token_weight[s] * row_scale[s] * row_scale[s] * (scale / width)
            line = jnp.sum(jnp.where(wide_eye, coef, 0.0), axis=0, keepdims=True)
            lines = lines + jnp.where(row8 == s, line, 0.0)
        coef_mine[...] = lines
        across().start()

    for i in peers:
        pltpu.make_async_remote_copy(
            src_ref=frag_recv.at[i], dst_ref=frag_recv.at[i], send_sem=frag_send.at[i],
            recv_sem=frag_got.at[i], device_id=(i, me), device_id_type=MESH).wait_recv()
    local[2].wait()
    local[3].wait()
    base = anchor_ref[...].astype(F32)
    delta = base - frag_recv[0].astype(F32)
    for i in range(1, replicas):
        delta = delta + (base - frag_recv[i].astype(F32))
    mean_delta = delta / replicas
    new_moment = NESTEROV * moment_ref[...].astype(F32) + mean_delta
    frag_all[my_frag, :] = base - OUTER_RATE * (mean_delta + NESTEROV * new_moment)

    def all_copy(i):
        return pltpu.make_async_remote_copy(
            src_ref=frag_all.at[my_frag, :], dst_ref=frag_all.at[my_frag, :],
            send_sem=all_send.at[i], recv_sem=all_got.at[rep],
            device_id=(i, me), device_id_type=MESH)

    for i in peers:
        all_copy(i).start()

    local[6 + units].wait()

    if paired:
        across().wait_recv()
        for s in range(steps):
            line = jnp.broadcast_to(coef_got[s:s + 1, :], (tokens, LANES))
            column = jnp.sum(jnp.where(wide_eye, line, 0.0), axis=1, keepdims=True)
            coef_across[s] = jnp.broadcast_to(column, (tokens, LANES))

    def part_copy(u, j):
        return pltpu.make_async_remote_copy(
            src_ref=part_send.at[u, block(j, few), :], dst_ref=part_recv.at[u, my_tokens, :],
            send_sem=part_send_sem.at[u, j], recv_sem=part_recv_sem.at[u, me],
            device_id=(rep, j), device_id_type=MESH)

    def grad_rows(u, first_row, size):
        start = u % parts * together + first_row * size
        return grads.at[u // parts, pl.ds(pl.multiple_of(start, size), size), :]

    def grad_copy(u, j):
        mine = grad_rows(u, me, few)
        return pltpu.make_async_remote_copy(
            src_ref=mine, dst_ref=mine, send_sem=grad_send.at[u, j],
            recv_sem=grad_recv.at[u, me], device_id=(rep, j), device_id_type=MESH)

    side, half = lax.rem(me, 2), me // 2
    mate, cross = me + 1 - 2 * side, lax.rem(me + 2, n)
    my_side, mate_side = block(side, 2 * few), block(1 - side, 2 * few)

    def pair_copy(kind, u):
        if kind == 0:
            src, dst, to = part_send.at[u, mate_side, :], part_recv.at[u, 0:2 * few, :], mate
        elif kind == 1:
            src, dst, to = part_send.at[u, my_side, :], part_recv.at[u, 2 * few:4 * few, :], cross
        else:
            src = dst = grad_rows(u, side, 2 * few)
            to = mate
        return pltpu.make_async_remote_copy(
            src_ref=src, dst_ref=dst, send_sem=part_send_sem.at[u, kind],
            recv_sem=part_recv_sem.at[u, kind], device_id=(rep, to), device_id_type=MESH)

    def pair_back(u):
        theirs = grad_rows(u, 1 - side, 2 * few)
        pltpu.make_async_remote_copy(
            src_ref=theirs, dst_ref=theirs, send_sem=part_send_sem.at[u, 2],
            recv_sem=part_recv_sem.at[u, 2], device_id=(rep, mate),
            device_id_type=MESH).wait_recv()

    tile = 256

    def project_and_share(u, held):
        s, q = u // parts, u % parts
        for j in others:
            a2a_arrived(u, j)
        local[6 + u].wait()

        @pl.loop(0, width // tile)
        def _(c):
            at = block(c, tile)
            out = jnp.dot(cols[u], held[:, at], preferred_element_type=F32)
            partial[:, at] = out
            part_send[u, :, at] = out.astype(BF16)

        if paired:
            pair_copy(0, u).start()
        else:
            for j in others:
                part_copy(u, j).start()

        @pl.loop(0, rows // tile)
        def _(c):
            at = block(c, tile)
            turned[s, at, q * together:(q + 1) * together] = cols[u, :, at].T

        few_rows = slice(q * few, (q + 1) * few)
        gain = row_scale[s, few_rows, :][:, :1]
        weight = token_weight[s, few_rows, :][:, :1]
        goal = targets[0, s, few_rows, :].astype(F32)
        if paired:
            share = weight * gain / width
            mine, theirs = block(half, few), block(1 - half, few)
            pair_copy(0, u).wait_recv()
            near = (partial[my_tokens, :] + part_recv[u, mine, :].astype(F32)) * (share * gain * scale)
            near = near - share * goal
            far = partial[block(slot(cross), few), :] + part_recv[u, theirs, :].astype(F32)
            far = far * coef_across[s, few_rows, :][:, :1]
            part_send[u, my_tokens, :] = near.astype(BF16)
            part_send[u, block(slot(cross), few), :] = far.astype(BF16)
            pair_copy(1, u).start()
            pair_copy(1, u).wait_recv()
            base = 2 * few
            near = near + part_recv[u, pl.ds(pl.multiple_of(base + half * few, few), few), :].astype(F32)
            far = far + part_recv[u, pl.ds(pl.multiple_of(base + (1 - half) * few, few), few), :].astype(F32)
            start = q * together
            grads[s, pl.ds(pl.multiple_of(start + slot(me) * few, few), few), :] = near.astype(BF16)
            grads[s, pl.ds(pl.multiple_of(start + slot(cross) * few, few), few), :] = far.astype(BF16)
            pair_copy(2, u).start()
            error = near / share
        else:
            values = partial[my_tokens, :]
            for j in others:
                at = block(j, few)
                pltpu.make_async_remote_copy(
                    src_ref=part_recv.at[u, at, :], dst_ref=part_recv.at[u, at, :],
                    send_sem=part_send_sem.at[u, j], recv_sem=part_recv_sem.at[u, j],
                    device_id=(rep, j), device_id_type=MESH).wait_recv()
                values = values + part_recv[u, at, :].astype(F32)
            error = values * (gain * scale) - goal
            start = q * together + me * few
            grads[s, pl.ds(pl.multiple_of(start, few), few), :] = (
                (weight * gain / width) * error).astype(BF16)
            for j in others:
                grad_copy(u, j).start()
        loss = jnp.sum(weight * 0.5 * jnp.mean(error * error, axis=-1, keepdims=True))
        loss = jnp.where(row8 == s, loss, 0.0)
        if u == 0:
            losses[me] = loss
        else:
            losses[me] = losses[me] + loss
        if u == units - 1:
            for j in others:
                to_all(losses, loss_send, loss_recv, j).start()
        if paired:
            pair_back(u)
        else:
            for j in others:
                theirs = grad_rows(u, j, few)
                pltpu.make_async_remote_copy(
                    src_ref=theirs, dst_ref=theirs, send_sem=grad_send.at[u, j],
                    recv_sem=grad_recv.at[u, j], device_id=(rep, j),
                    device_id_type=MESH).wait_recv()

    for u in range(parts):
        for j in others:
            a2a(u, j).wait_send()
            if u + 2 < units:
                a2a(u + 2, j).start()
        project_and_share(u, w_ref)
    local[4].wait()
    local[5].wait()
    rt = 128

    for i in peers:
        at = block(i, own)
        pltpu.make_async_remote_copy(
            src_ref=frag_all.at[at, :], dst_ref=frag_all.at[at, :], send_sem=all_send.at[i],
            recv_sem=all_got.at[i], device_id=(i, me), device_id_type=MESH).wait_recv()

    @pl.loop(0, rows // rt)
    def _(c):
        at = block(c, rt)
        gradient = jnp.dot(turned[0, at, :], grads[0], preferred_element_type=F32) * scale
        new_master, new_first, new_second = adam_update(
            w_ref[at, :].astype(F32), m_ref[at, :].astype(F32), v_ref[at, :].astype(F32), gradient)
        current[at, :] = new_master.astype(BF16)
        first[at, :] = (INNER_RATE * BETA_FIRST) * new_first
        second[at, :] = BETA_SECOND * new_second
        kept = (1.0 - INNER_RATE * DECAY_RATE) * new_master
        mixed = (1.0 - MIXING) * frag_all[at, :]
        for k in range(width // fw):
            piece = kept[:, k * fw:(k + 1) * fw]
            master[at, k * fw:(k + 1) * fw] = jnp.where(picked == k, MIXING * piece + mixed, piece)

    for u in range(parts, units):
        if u + 2 < units:
            for j in others:
                a2a(u, j).wait_send()
                a2a(u + 2, j).start()
        project_and_share(u, current)
    for j in others:
        from_all(losses, loss_send, loss_recv, j)
    loss = losses[0]
    for j in range(1, n):
        loss = loss + losses[j]
    loss_out[...] = loss

    for j in others:
        for u in range(parts, units):
            if u + 2 >= units:
                a2a(u, j).wait_send()
        to_all(counts, count_send, count_recv, j).wait_send()
        to_all(losses, loss_send, loss_recv, j).wait_send()
        if not paired:
            for u in range(units):
                part_copy(u, j).wait_send()
                grad_copy(u, j).wait_send()
    if paired:
        across().wait_send()
        for u in range(units):
            for kind in range(3):
                pair_copy(kind, u).wait_send()
    for i in peers:
        frag_copy(i).wait_send()
        all_copy(i).wait_send()


def finish_kernel(scale, fw, fragment, kept, first, second, turned, grads, loss, out, loss_out,
                  done, out_sem):
    rows, width = kept.shape
    last = turned.shape[0] - 1
    tiles = out_sem.shape[0]
    rt = rows // tiles
    column = lax.broadcasted_iota(jnp.int32, (1, width), 1) // fw
    share = jnp.where(column == fragment[0], MIXING, 1.0)

    def write(c):
        at = pl.ds(pl.multiple_of(c * rt, rt), rt)
        return pltpu.make_async_copy(done.at[at, :], out.at[0, at, :], out_sem.at[c])

    @pl.loop(0, tiles)
    def _(c):
        at = pl.ds(pl.multiple_of(c * rt, rt), rt)
        raw = jnp.dot(turned[last, at, :], grads[last], preferred_element_type=F32)
        moved = first[at, :] + (INNER_RATE * (1.0 - BETA_FIRST) * scale) * raw
        power = second[at, :] + ((1.0 - BETA_SECOND) * scale * scale) * (raw * raw)
        step = moved / (power * lax.rsqrt(power) + ADAM_EPS)
        done[at, :] = kept[at, :] - share * step
        write(c).start()

    steps = loss_out.shape[1]
    across = lax.broadcasted_iota(jnp.int32, (1, steps), 1)
    line = jnp.zeros((1, steps), F32)
    for s in range(steps):
        line = jnp.where(across == s, loss[s:s + 1, :steps], line)
    loss_out[...] = line

    @pl.loop(0, tiles)
    def _(c):
        write(c).wait()


def body(n, replicas, hidden, targets, doc_ids, weights, adam_m, adam_v, anchor, momentum, fragment):
    steps, tokens, model = hidden.shape[1:]
    rows, width = weights.shape[1:]
    fw = anchor.shape[1]
    own = rows // replicas
    everyone = n * tokens
    parts = 2 if tokens % 32 == 0 else 1
    units = steps * parts
    together = everyone // parts
    dims = (steps, tokens, rows, width, model, fw)
    any_spec = pl.BlockSpec(memory_space=pltpu.HBM)
    vmem = pl.BlockSpec(memory_space=pltpu.VMEM)
    smem = pl.BlockSpec(memory_space=pltpu.SMEM)
    dma = pltpu.SemaphoreType.DMA
    shape = jax.ShapeDtypeStruct
    outer = [pltpu.with_memory_space_constraint(x, pltpu.HBM) for x in (
        hidden, targets, doc_ids, weights, adam_m, adam_v, anchor, momentum)]
    master, first, second, turned, grads, loss = pl.pallas_call(
        functools.partial(window_kernel, n, replicas, dims),
        out_shape=[
            pltpu.VMEM((rows, width), F32), pltpu.VMEM((rows, width), F32),
            pltpu.VMEM((rows, width), F32), pltpu.VMEM((steps, rows, everyone), BF16),
            pltpu.VMEM((steps, everyone, width), BF16), pltpu.VMEM((8, LANES), F32),
        ],
        in_specs=[any_spec] * 8 + [smem],
        out_specs=[vmem] * 6,
        scratch_shapes=[
            pltpu.VMEM((units, together, rows), BF16),
            pltpu.VMEM((steps, tokens, model), BF16),
            pltpu.VMEM((1, steps, tokens, width), BF16),
            pltpu.VMEM((1, steps, tokens), jnp.int32),
            pltpu.VMEM((rows, width), BF16),
            pltpu.VMEM((rows, width), BF16),
            pltpu.VMEM((rows, width), BF16),
            pltpu.VMEM((rows, width), BF16),
            pltpu.VMEM((together, width), F32),
            pltpu.VMEM((units, together, width), BF16),
            pltpu.VMEM((units, together, width), BF16),
            pltpu.VMEM((n, 8, LANES), F32),
            pltpu.VMEM((n, 8, LANES), F32),
            pltpu.VMEM((rows, fw), BF16),
            pltpu.VMEM((replicas, own, fw), BF16),
            pltpu.VMEM((rows, fw), F32),
            pltpu.VMEM((own, fw), BF16),
            pltpu.VMEM((own, fw), BF16),
            pltpu.VMEM((steps, tokens, LANES), F32),
            pltpu.VMEM((steps, tokens, LANES), F32),
            pltpu.VMEM((8, LANES), F32),
            pltpu.VMEM((8, LANES), F32),
            pltpu.VMEM((steps, tokens, LANES), F32),
            dma((2,)),
            dma((8 + units,)),
            dma((units, n)), dma((units, n)), dma((n,)), dma((n,)),
            dma((replicas,)), dma((replicas,)), dma((replicas,)), dma((replicas,)),
            dma((units, n)), dma((units, n)),
            dma((units, n)), dma((units, n)), dma((n,)), dma((n,)),
        ],
        compiler_params=pltpu.CompilerParams(
            collective_id=0, has_side_effects=True, vmem_limit_bytes=28 * 1024 * 1024),
        name="window",
    )(*outer, fragment)

    inner = [pltpu.with_memory_space_constraint(x, pltpu.VMEM)
             for x in (master, first, second, turned, grads, loss)]
    return pl.pallas_call(
        functools.partial(finish_kernel, model ** (-0.5), fw),
        out_shape=[shape((1, rows, width), F32), shape((1, steps), F32)],
        in_specs=[smem] + [vmem] * 6,
        out_specs=[any_spec, vmem],
        scratch_shapes=[pltpu.VMEM((rows, width), F32), dma((8,))],
        compiler_params=pltpu.CompilerParams(vmem_limit_bytes=16 * 1024 * 1024),
        name="finish",
    )(fragment, *inner)


def solution(mesh):
    placed = (
        P("replica", None, "fsdp", None),
        P("replica", None, "fsdp", None),
        P("replica", None, "fsdp"),
        P("replica", "fsdp", None),
        P("replica", "fsdp", None),
        P("replica", "fsdp", None),
        P("fsdp", None),
        P("fsdp", None),
        P(),
    )
    return jax.shard_map(
        functools.partial(body, mesh.shape["fsdp"], mesh.shape["replica"]),
        mesh=mesh,
        in_specs=placed,
        out_specs=(P("replica", "fsdp", None), P("replica", None)),
        check_vma=False,
    )
```

```python
import functools

import jax
import jax.numpy as jnp
from jax import lax
from jax.experimental import pallas as pl
from jax.experimental.pallas import tpu as pltpu
from jax.sharding import PartitionSpec as P

DOCS = 8
NORM_EPS = 1e-05
ADAM_EPS = 1e-08
INNER_RATE = 0.1
DECAY_RATE = 0.1
BETA_FIRST = 0.9
BETA_SECOND = 0.95
OUTER_RATE = 0.7
NESTEROV = 0.9
MIXING = 0.5
LANES = 128
MESH = pl.DeviceIdType.MESH
F32 = jnp.float32
BF16 = jnp.bfloat16


def adam_update(master, first, second, gradient):
    first = BETA_FIRST * first + (1.0 - BETA_FIRST) * gradient
    second = BETA_SECOND * second + (1.0 - BETA_SECOND) * gradient * gradient
    master = master - INNER_RATE * (first / (jnp.sqrt(second) + ADAM_EPS) + DECAY_RATE * master)
    return (master, first, second)


def partners(me, n):
    if n == 4:
        return [lax.rem(me + 2, 4), 3 - me, me + 1 - 2 * lax.rem(me, 2)]
    return [lax.rem(me + k, n) for k in range(1, n)]


def window_kernel(
    n, replicas, dims,
    hidden, targets_in, ids_in, weights, adam_m, adam_v, anchor, momentum, fragment,
    master, first, second, turned, grads, loss_out,
    cols, hid, targets, doc_ids, w_ref, m_ref, v_ref, current,
    partial, part_send, part_recv, counts, losses,
    frag_cols, frag_recv, frag_all, anchor_ref, moment_ref, row_scale, token_weight,
    coef_mine, coef_got, coef_across, coef_sem,
    local_sem, a2a_send, a2a_recv, count_send, count_recv,
    frag_send, frag_got, all_send, all_got, part_send_sem, part_recv_sem,
    grad_send, grad_recv, loss_send, loss_recv,
):
    steps, tokens, rows, width, model, fw = dims
    paired = n == 4 and tokens <= LANES
    units = cols.shape[0]
    parts = units // steps
    few = tokens // parts
    together = n * few
    own = rows // replicas
    scale = model ** (-0.5)
    rep = lax.axis_index("replica")
    me = lax.axis_index("fsdp")
    others = partners(me, n)
    peers = [lax.rem(rep + k, replicas) for k in range(1, replicas)]

    def block(index, size):
        return pl.ds(pl.multiple_of(index * size, size), size)

    def slot(j):
        return 2 * lax.rem(j, 2) + j // 2 if paired else j

    my_tokens = block(slot(me), few)
    my_frag = block(rep, own)

    local = [
        pltpu.make_async_copy(weights.at[0], w_ref, local_sem.at[0]),
        pltpu.make_async_copy(hidden.at[0], hid, local_sem.at[1]),
        pltpu.make_async_copy(anchor.at[my_frag, :], anchor_ref, local_sem.at[2]),
        pltpu.make_async_copy(momentum.at[my_frag, :], moment_ref, local_sem.at[3]),
        pltpu.make_async_copy(adam_m.at[0], m_ref, local_sem.at[4]),
        pltpu.make_async_copy(adam_v.at[0], v_ref, local_sem.at[5]),
    ]

    def held_tokens(u, j):
        return hidden.at[0, u // parts, u % parts * few:(u % parts + 1) * few, block(j, rows)]

    for u in range(units):
        local.append(pltpu.make_async_copy(
            held_tokens(u, me), cols.at[u, my_tokens, :], local_sem.at[6 + u]))
    local.append(pltpu.make_async_copy(targets_in, targets, local_sem.at[6 + units]))
    local.append(pltpu.make_async_copy(ids_in, doc_ids, local_sem.at[7 + units]))
    for copy in local:
        copy.start()

    barrier = pltpu.get_barrier_semaphore()
    for j in others:
        pl.semaphore_signal(barrier, inc=1, device_id=(rep, j), device_id_type=MESH)
    for i in peers:
        pl.semaphore_signal(barrier, inc=1, device_id=(i, me), device_id_type=MESH)
    pl.semaphore_wait(barrier, n + replicas - 2)

    def a2a(u, j):
        return pltpu.make_async_remote_copy(
            src_ref=held_tokens(u, j), dst_ref=cols.at[u, my_tokens, :],
            send_sem=a2a_send.at[u, j], recv_sem=a2a_recv.at[u, me],
            device_id=(rep, j), device_id_type=MESH)

    def a2a_arrived(u, j):
        pltpu.make_async_remote_copy(
            src_ref=held_tokens(u, j), dst_ref=cols.at[u, block(slot(j), few), :],
            send_sem=a2a_send.at[u, j], recv_sem=a2a_recv.at[u, j],
            device_id=(rep, j), device_id_type=MESH).wait_recv()

    for u in range(parts):
        for j in others:
            a2a(u, j).start()

    local[7 + units].wait()
    lane = lax.broadcasted_iota(jnp.int32, (tokens, LANES), 1).astype(F32)
    eye = (lax.broadcasted_iota(jnp.int32, (tokens, tokens), 0)
           == lax.broadcasted_iota(jnp.int32, (tokens, tokens), 1))
    wide_eye = (lax.broadcasted_iota(jnp.int32, (tokens, LANES), 0)
                == lax.broadcasted_iota(jnp.int32, (tokens, LANES), 1))
    onehots = []
    row8 = lax.broadcasted_iota(jnp.int32, (8, LANES), 0)
    tally = jnp.zeros((8, LANES), F32)
    for s in range(steps):
        ids = jnp.broadcast_to(doc_ids[0, s:s + 1, :].astype(F32), (tokens, tokens))
        ids = jnp.sum(jnp.where(eye, ids, 0.0), axis=1, keepdims=True)
        onehot = (ids == lane).astype(F32)
        onehots.append(onehot)
        tally = tally + jnp.where(row8 == s, jnp.sum(onehot, axis=0, keepdims=True), 0.0)
    counts[me] = tally

    def to_all(buf, send, recv, j):
        return pltpu.make_async_remote_copy(
            src_ref=buf.at[me], dst_ref=buf.at[me], send_sem=send.at[j], recv_sem=recv.at[me],
            device_id=(rep, j), device_id_type=MESH)

    def from_all(buf, send, recv, j):
        pltpu.make_async_remote_copy(
            src_ref=buf.at[j], dst_ref=buf.at[j], send_sem=send.at[j], recv_sem=recv.at[j],
            device_id=(rep, j), device_id_type=MESH).wait_recv()

    for j in others:
        to_all(counts, count_send, count_recv, j).start()

    local[0].wait()
    picked = fragment[0]
    for k in range(width // fw):
        piece = w_ref[:, k * fw:(k + 1) * fw]
        if k == 0:
            frag_cols[...] = piece
        else:
            frag_cols[...] = jnp.where(picked == k, piece, frag_cols[...])

    def frag_copy(i):
        return pltpu.make_async_remote_copy(
            src_ref=frag_cols.at[block(i, own), :], dst_ref=frag_recv.at[rep],
            send_sem=frag_send.at[i], recv_sem=frag_got.at[rep],
            device_id=(i, me), device_id_type=MESH)

    for i in peers:
        frag_copy(i).start()
    frag_recv[rep] = frag_cols[my_frag, :]

    local[1].wait()
    wide = 4 * LANES
    for s in range(steps):
        def add_squares(c, acc, s=s):
            x = hid[s, :, block(c, wide)].astype(F32)
            return acc + x * x
        acc = lax.fori_loop(0, model // wide, add_squares, jnp.zeros((tokens, wide), F32))
        power = jnp.sum(acc, axis=1, keepdims=True) / model
        row_scale[s] = jnp.broadcast_to(lax.rsqrt(power + NORM_EPS), (tokens, LANES))

    for j in others:
        from_all(counts, count_send, count_recv, j)
    total = counts[0]
    for j in range(1, n):
        total = total + counts[j]
    inverse = jnp.where(total > 0.0, 1.0 / (DOCS * jnp.maximum(total, 1.0)), 0.0)
    for s in range(steps):
        weight = jnp.sum(onehots[s] * inverse[s:s + 1, :], axis=1, keepdims=True)
        token_weight[s] = jnp.broadcast_to(weight, (tokens, LANES))

    def across():
        return pltpu.make_async_remote_copy(
            src_ref=coef_mine, dst_ref=coef_got, send_sem=coef_sem.at[0], recv_sem=coef_sem.at[1],
            device_id=(rep, lax.rem(me + 2, n)), device_id_type=MESH)

    if paired:
        lines = jnp.zeros((8, LANES), F32)
        for s in range(steps):
            coef = token_weight[s] * row_scale[s] * row_scale[s] * (scale / width)
            line = jnp.sum(jnp.where(wide_eye, coef, 0.0), axis=0, keepdims=True)
            lines = lines + jnp.where(row8 == s, line, 0.0)
        coef_mine[...] = lines
        across().start()

    for i in peers:
        pltpu.make_async_remote_copy(
            src_ref=frag_recv.at[i], dst_ref=frag_recv.at[i], send_sem=frag_send.at[i],
            recv_sem=frag_got.at[i], device_id=(i, me), device_id_type=MESH).wait_recv()
    local[2].wait()
    local[3].wait()
    base = anchor_ref[...].astype(F32)
    delta = base - frag_recv[0].astype(F32)
    for i in range(1, replicas):
        delta = delta + (base - frag_recv[i].astype(F32))
    mean_delta = delta / replicas
    new_moment = NESTEROV * moment_ref[...].astype(F32) + mean_delta
    frag_all[my_frag, :] = base - OUTER_RATE * (mean_delta + NESTEROV * new_moment)

    def all_copy(i):
        return pltpu.make_async_remote_copy(
            src_ref=frag_all.at[my_frag, :], dst_ref=frag_all.at[my_frag, :],
            send_sem=all_send.at[i], recv_sem=all_got.at[rep],
            device_id=(i, me), device_id_type=MESH)

    for i in peers:
        all_copy(i).start()

    local[6 + units].wait()

    if paired:
        across().wait_recv()
        for s in range(steps):
            line = jnp.broadcast_to(coef_got[s:s + 1, :], (tokens, LANES))
            column = jnp.sum(jnp.where(wide_eye, line, 0.0), axis=1, keepdims=True)
            coef_across[s] = jnp.broadcast_to(column, (tokens, LANES))

    def part_copy(u, j):
        return pltpu.make_async_remote_copy(
            src_ref=part_send.at[u, block(j, few), :], dst_ref=part_recv.at[u, my_tokens, :],
            send_sem=part_send_sem.at[u, j], recv_sem=part_recv_sem.at[u, me],
            device_id=(rep, j), device_id_type=MESH)

    def grad_rows(u, first_row, size):
        start = u % parts * together + first_row * size
        return grads.at[u // parts, pl.ds(pl.multiple_of(start, size), size), :]

    def grad_copy(u, j):
        mine = grad_rows(u, me, few)
        return pltpu.make_async_remote_copy(
            src_ref=mine, dst_ref=mine, send_sem=grad_send.at[u, j],
            recv_sem=grad_recv.at[u, me], device_id=(rep, j), device_id_type=MESH)

    side, half = lax.rem(me, 2), me // 2
    mate, cross = me + 1 - 2 * side, lax.rem(me + 2, n)
    my_side, mate_side = block(side, 2 * few), block(1 - side, 2 * few)

    def pair_copy(kind, u):
        if kind == 0:
            src, dst, to = part_send.at[u, mate_side, :], part_recv.at[u, 0:2 * few, :], mate
        elif kind == 1:
            src, dst, to = part_send.at[u, my_side, :], part_recv.at[u, 2 * few:4 * few, :], cross
        else:
            src = dst = grad_rows(u, side, 2 * few)
            to = mate
        return pltpu.make_async_remote_copy(
            src_ref=src, dst_ref=dst, send_sem=part_send_sem.at[u, kind],
            recv_sem=part_recv_sem.at[u, kind], device_id=(rep, to), device_id_type=MESH)

    def pair_back(u):
        theirs = grad_rows(u, 1 - side, 2 * few)
        pltpu.make_async_remote_copy(
            src_ref=theirs, dst_ref=theirs, send_sem=part_send_sem.at[u, 2],
            recv_sem=part_recv_sem.at[u, 2], device_id=(rep, mate),
            device_id_type=MESH).wait_recv()

    tile = 256

    def factors(u):
        s, q = u // parts, u % parts
        few_rows = slice(q * few, (q + 1) * few)
        gain = row_scale[s, few_rows, :][:, :1]
        weight = token_weight[s, few_rows, :][:, :1]
        return s, q, few_rows, gain, weight

    def project(u, held):
        s, q = u // parts, u % parts
        for j in others:
            a2a_arrived(u, j)
        local[6 + u].wait()

        @pl.loop(0, width // tile)
        def _(c):
            at = block(c, tile)
            out = jnp.dot(cols[u], held[:, at], preferred_element_type=F32)
            partial[u, :, at] = out
            part_send[u, :, at] = out.astype(BF16)

        if paired:
            pair_copy(0, u).start()
        else:
            for j in others:
                part_copy(u, j).start()

        @pl.loop(0, rows // tile)
        def _(c):
            at = block(c, tile)
            turned[s, at, q * together:(q + 1) * together] = cols[u, :, at].T

    def join_mate(u):
        if not paired:
            return
        s, q, few_rows, gain, weight = factors(u)
        share = weight * gain / width
        goal = targets[0, s, few_rows, :].astype(F32)
        mine, theirs = block(half, few), block(1 - half, few)
        other_rows = block(slot(cross), few)
        pair_copy(0, u).wait_recv()
        near = partial[u, my_tokens, :] + part_recv[u, mine, :].astype(F32)
        near = near * (share * gain * scale) - share * goal
        far = partial[u, other_rows, :] + part_recv[u, theirs, :].astype(F32)
        far = far * coef_across[s, few_rows, :][:, :1]
        part_send[u, my_tokens, :] = near.astype(BF16)
        part_send[u, other_rows, :] = far.astype(BF16)
        pair_copy(1, u).start()
        partial[u, my_tokens, :] = near
        partial[u, other_rows, :] = far

    def join_across(u):
        s, q, few_rows, gain, weight = factors(u)
        start = q * together
        if paired:
            share = weight * gain / width
            other_rows = block(slot(cross), few)
            base = 2 * few
            pair_copy(1, u).wait_recv()
            near = partial[u, my_tokens, :] + part_recv[
                u, pl.ds(pl.multiple_of(base + half * few, few), few), :].astype(F32)
            far = partial[u, other_rows, :] + part_recv[
                u, pl.ds(pl.multiple_of(base + (1 - half) * few, few), few), :].astype(F32)
            grads[s, pl.ds(pl.multiple_of(start + slot(me) * few, few), few), :] = near.astype(BF16)
            grads[s, pl.ds(pl.multiple_of(start + slot(cross) * few, few), few), :] = far.astype(BF16)
            pair_copy(2, u).start()
            error = near / share
        else:
            values = partial[u, my_tokens, :]
            for j in others:
                at = block(j, few)
                pltpu.make_async_remote_copy(
                    src_ref=part_recv.at[u, at, :], dst_ref=part_recv.at[u, at, :],
                    send_sem=part_send_sem.at[u, j], recv_sem=part_recv_sem.at[u, j],
                    device_id=(rep, j), device_id_type=MESH).wait_recv()
                values = values + part_recv[u, at, :].astype(F32)
            error = values * (gain * scale) - targets[0, s, few_rows, :].astype(F32)
            grads[s, pl.ds(pl.multiple_of(start + me * few, few), few), :] = (
                (weight * gain / width) * error).astype(BF16)
            for j in others:
                grad_copy(u, j).start()
        loss = jnp.sum(weight * 0.5 * jnp.mean(error * error, axis=-1, keepdims=True))
        loss = jnp.where(row8 == s, loss, 0.0)
        if u == 0:
            losses[me] = loss
        else:
            losses[me] = losses[me] + loss
        if u == units - 1:
            for j in others:
                to_all(losses, loss_send, loss_recv, j).start()

    def join_all(u):
        if paired:
            pair_back(u)
        else:
            for j in others:
                theirs = grad_rows(u, j, few)
                pltpu.make_async_remote_copy(
                    src_ref=theirs, dst_ref=theirs, send_sem=grad_send.at[u, j],
                    recv_sem=grad_recv.at[u, j], device_id=(rep, j),
                    device_id_type=MESH).wait_recv()

    now, later = range(parts), range(parts, units)
    queue = [(u, j) for u in later for j in others]
    for j in others:
        for u in now:
            a2a(u, j).wait_send()
    a2a(*queue[0]).start()
    for u in now:
        project(u, w_ref)
    for u in now:
        join_mate(u)
    a2a(*queue[1]).start()
    for u in now:
        join_across(u)
    for u, j in queue[2:]:
        a2a(u, j).start()
    for u in now:
        join_all(u)
    local[4].wait()
    local[5].wait()
    rt = 128

    for i in peers:
        at = block(i, own)
        pltpu.make_async_remote_copy(
            src_ref=frag_all.at[at, :], dst_ref=frag_all.at[at, :], send_sem=all_send.at[i],
            recv_sem=all_got.at[i], device_id=(i, me), device_id_type=MESH).wait_recv()

    @pl.loop(0, rows // rt)
    def _(c):
        at = block(c, rt)
        gradient = jnp.dot(turned[0, at, :], grads[0], preferred_element_type=F32) * scale
        new_master, new_first, new_second = adam_update(
            w_ref[at, :].astype(F32), m_ref[at, :].astype(F32), v_ref[at, :].astype(F32), gradient)
        current[at, :] = new_master.astype(BF16)
        first[at, :] = (INNER_RATE * BETA_FIRST) * new_first
        second[at, :] = BETA_SECOND * new_second
        kept = (1.0 - INNER_RATE * DECAY_RATE) * new_master
        mixed = (1.0 - MIXING) * frag_all[at, :]
        for k in range(width // fw):
            piece = kept[:, k * fw:(k + 1) * fw]
            master[at, k * fw:(k + 1) * fw] = jnp.where(picked == k, MIXING * piece + mixed, piece)

    stages = [lambda u: project(u, current), join_mate, join_across, join_all]
    for turn in range(2 * (parts - 1) + len(stages)):
        for i, u in reversed(list(enumerate(later))):
            if 0 <= turn - 2 * i < len(stages):
                stages[turn - 2 * i](u)
    for j in others:
        from_all(losses, loss_send, loss_recv, j)
    loss = losses[0]
    for j in range(1, n):
        loss = loss + losses[j]
    loss_out[...] = loss

    for j in others:
        for u in range(parts, units):
            a2a(u, j).wait_send()
        to_all(counts, count_send, count_recv, j).wait_send()
        to_all(losses, loss_send, loss_recv, j).wait_send()
        if not paired:
            for u in range(units):
                part_copy(u, j).wait_send()
                grad_copy(u, j).wait_send()
    if paired:
        across().wait_send()
        for u in range(units):
            for kind in range(3):
                pair_copy(kind, u).wait_send()
    for i in peers:
        frag_copy(i).wait_send()
        all_copy(i).wait_send()


def finish_kernel(scale, fw, fragment, kept, first, second, turned, grads, loss, out, loss_out,
                  done, out_sem):
    rows, width = kept.shape
    last = turned.shape[0] - 1
    tiles = out_sem.shape[0]
    rt = rows // tiles
    column = lax.broadcasted_iota(jnp.int32, (1, width), 1) // fw
    share = jnp.where(column == fragment[0], MIXING, 1.0)

    def write(c):
        at = pl.ds(pl.multiple_of(c * rt, rt), rt)
        return pltpu.make_async_copy(done.at[at, :], out.at[0, at, :], out_sem.at[c])

    @pl.loop(0, tiles)
    def _(c):
        at = pl.ds(pl.multiple_of(c * rt, rt), rt)
        raw = jnp.dot(turned[last, at, :], grads[last], preferred_element_type=F32)
        moved = first[at, :] + (INNER_RATE * (1.0 - BETA_FIRST) * scale) * raw
        power = second[at, :] + ((1.0 - BETA_SECOND) * scale * scale) * (raw * raw)
        step = moved / (power * lax.rsqrt(power) + ADAM_EPS)
        done[at, :] = kept[at, :] - share * step
        write(c).start()

    steps = loss_out.shape[1]
    across = lax.broadcasted_iota(jnp.int32, (1, steps), 1)
    line = jnp.zeros((1, steps), F32)
    for s in range(steps):
        line = jnp.where(across == s, loss[s:s + 1, :steps], line)
    loss_out[...] = line

    @pl.loop(0, tiles)
    def _(c):
        write(c).wait()


def body(n, replicas, hidden, targets, doc_ids, weights, adam_m, adam_v, anchor, momentum, fragment):
    steps, tokens, model = hidden.shape[1:]
    rows, width = weights.shape[1:]
    fw = anchor.shape[1]
    own = rows // replicas
    everyone = n * tokens
    parts = 2 if tokens % 32 == 0 else 1
    units = steps * parts
    together = everyone // parts
    dims = (steps, tokens, rows, width, model, fw)
    any_spec = pl.BlockSpec(memory_space=pltpu.HBM)
    vmem = pl.BlockSpec(memory_space=pltpu.VMEM)
    smem = pl.BlockSpec(memory_space=pltpu.SMEM)
    dma = pltpu.SemaphoreType.DMA
    shape = jax.ShapeDtypeStruct
    outer = [pltpu.with_memory_space_constraint(x, pltpu.HBM) for x in (
        hidden, targets, doc_ids, weights, adam_m, adam_v, anchor, momentum)]
    master, first, second, turned, grads, loss = pl.pallas_call(
        functools.partial(window_kernel, n, replicas, dims),
        out_shape=[
            pltpu.VMEM((rows, width), F32), pltpu.VMEM((rows, width), F32),
            pltpu.VMEM((rows, width), F32), pltpu.VMEM((steps, rows, everyone), BF16),
            pltpu.VMEM((steps, everyone, width), BF16), pltpu.VMEM((8, LANES), F32),
        ],
        in_specs=[any_spec] * 8 + [smem],
        out_specs=[vmem] * 6,
        scratch_shapes=[
            pltpu.VMEM((units, together, rows), BF16),
            pltpu.VMEM((steps, tokens, model), BF16),
            pltpu.VMEM((1, steps, tokens, width), BF16),
            pltpu.VMEM((1, steps, tokens), jnp.int32),
            pltpu.VMEM((rows, width), BF16),
            pltpu.VMEM((rows, width), BF16),
            pltpu.VMEM((rows, width), BF16),
            pltpu.VMEM((rows, width), BF16),
            pltpu.VMEM((units, together, width), F32),
            pltpu.VMEM((units, together, width), BF16),
            pltpu.VMEM((units, together, width), BF16),
            pltpu.VMEM((n, 8, LANES), F32),
            pltpu.VMEM((n, 8, LANES), F32),
            pltpu.VMEM((rows, fw), BF16),
            pltpu.VMEM((replicas, own, fw), BF16),
            pltpu.VMEM((rows, fw), F32),
            pltpu.VMEM((own, fw), BF16),
            pltpu.VMEM((own, fw), BF16),
            pltpu.VMEM((steps, tokens, LANES), F32),
            pltpu.VMEM((steps, tokens, LANES), F32),
            pltpu.VMEM((8, LANES), F32),
            pltpu.VMEM((8, LANES), F32),
            pltpu.VMEM((steps, tokens, LANES), F32),
            dma((2,)),
            dma((8 + units,)),
            dma((units, n)), dma((units, n)), dma((n,)), dma((n,)),
            dma((replicas,)), dma((replicas,)), dma((replicas,)), dma((replicas,)),
            dma((units, n)), dma((units, n)),
            dma((units, n)), dma((units, n)), dma((n,)), dma((n,)),
        ],
        compiler_params=pltpu.CompilerParams(
            collective_id=0, has_side_effects=True, vmem_limit_bytes=28 * 1024 * 1024),
        name="window",
    )(*outer, fragment)

    inner = [pltpu.with_memory_space_constraint(x, pltpu.VMEM)
             for x in (master, first, second, turned, grads, loss)]
    return pl.pallas_call(
        functools.partial(finish_kernel, model ** (-0.5), fw),
        out_shape=[shape((1, rows, width), F32), shape((1, steps), F32)],
        in_specs=[smem] + [vmem] * 6,
        out_specs=[any_spec, vmem],
        scratch_shapes=[pltpu.VMEM((rows, width), F32), dma((8,))],
        compiler_params=pltpu.CompilerParams(vmem_limit_bytes=16 * 1024 * 1024),
        name="finish",
    )(fragment, *inner)


def solution(mesh):
    placed = (
        P("replica", None, "fsdp", None),
        P("replica", None, "fsdp", None),
        P("replica", None, "fsdp"),
        P("replica", "fsdp", None),
        P("replica", "fsdp", None),
        P("replica", "fsdp", None),
        P("fsdp", None),
        P("fsdp", None),
        P(),
    )
    return jax.shard_map(
        functools.partial(body, mesh.shape["fsdp"], mesh.shape["replica"]),
        mesh=mesh,
        in_specs=placed,
        out_specs=(P("replica", "fsdp", None), P("replica", None)),
        check_vma=False,
    )
```

```python
import functools

import jax
import jax.numpy as jnp
from jax import lax
from jax.experimental import pallas as pl
from jax.experimental.pallas import tpu as pltpu
from jax.sharding import PartitionSpec as P

DOCS = 8
NORM_EPS = 1e-05
ADAM_EPS = 1e-08
INNER_RATE = 0.1
DECAY_RATE = 0.1
BETA_FIRST = 0.9
BETA_SECOND = 0.95
OUTER_RATE = 0.7
NESTEROV = 0.9
MIXING = 0.5
LANES = 128
MESH = pl.DeviceIdType.MESH
F32 = jnp.float32
BF16 = jnp.bfloat16


def adam_update(master, first, second, gradient):
    first = BETA_FIRST * first + (1.0 - BETA_FIRST) * gradient
    second = BETA_SECOND * second + (1.0 - BETA_SECOND) * gradient * gradient
    master = master - INNER_RATE * (first / (second * lax.rsqrt(second) + ADAM_EPS) + DECAY_RATE * master)
    return (master, first, second)


def partners(me, n):
    if n == 4:
        return [lax.rem(me + 2, 4), 3 - me, me + 1 - 2 * lax.rem(me, 2)]
    return [lax.rem(me + k, n) for k in range(1, n)]


def window_kernel(
    n, replicas, dims,
    hidden, targets_in, ids_in, weights, adam_m, adam_v, anchor, momentum, fragment,
    master, first, second, turned, grads, loss_out,
    cols, hid, targets, doc_ids, w_ref, m_ref, v_ref, current,
    partial, part_send, part_recv, counts, losses,
    frag_cols, frag_recv, frag_all, anchor_ref, moment_ref, row_scale, token_weight,
    coef_mine, coef_got, coef_across, coef_sem,
    local_sem, a2a_send, a2a_recv, count_send, count_recv,
    frag_send, frag_got, all_send, all_got, part_send_sem, part_recv_sem,
    grad_send, grad_recv, loss_send, loss_recv,
):
    steps, tokens, rows, width, model, fw = dims
    paired = n == 4 and tokens <= LANES
    units = cols.shape[0]
    parts = units // steps
    few = tokens // parts
    together = n * few
    own = rows // replicas
    scale = model ** (-0.5)
    rep = lax.axis_index("replica")
    me = lax.axis_index("fsdp")
    others = partners(me, n)
    peers = [lax.rem(rep + k, replicas) for k in range(1, replicas)]

    def block(index, size):
        return pl.ds(pl.multiple_of(index * size, size), size)

    def slot(j):
        return 2 * lax.rem(j, 2) + j // 2 if paired else j

    my_tokens = block(slot(me), few)
    my_frag = block(rep, own)

    local = [
        pltpu.make_async_copy(weights.at[0], w_ref, local_sem.at[0]),
        pltpu.make_async_copy(hidden.at[0], hid, local_sem.at[1]),
        pltpu.make_async_copy(anchor.at[my_frag, :], anchor_ref, local_sem.at[2]),
        pltpu.make_async_copy(momentum.at[my_frag, :], moment_ref, local_sem.at[3]),
        pltpu.make_async_copy(adam_m.at[0], m_ref, local_sem.at[4]),
        pltpu.make_async_copy(adam_v.at[0], v_ref, local_sem.at[5]),
    ]

    def held_tokens(u, j):
        return hidden.at[0, u // parts, u % parts * few:(u % parts + 1) * few, block(j, rows)]

    for u in range(units):
        local.append(pltpu.make_async_copy(
            held_tokens(u, me), cols.at[u, my_tokens, :], local_sem.at[6 + u]))
    local.append(pltpu.make_async_copy(targets_in, targets, local_sem.at[6 + units]))
    local.append(pltpu.make_async_copy(ids_in, doc_ids, local_sem.at[7 + units]))
    for copy in local:
        copy.start()

    local[7 + units].wait()
    lane = lax.broadcasted_iota(jnp.int32, (tokens, LANES), 1).astype(F32)
    eye = (lax.broadcasted_iota(jnp.int32, (tokens, tokens), 0)
           == lax.broadcasted_iota(jnp.int32, (tokens, tokens), 1))
    wide_eye = (lax.broadcasted_iota(jnp.int32, (tokens, LANES), 0)
                == lax.broadcasted_iota(jnp.int32, (tokens, LANES), 1))
    onehots = []
    row8 = lax.broadcasted_iota(jnp.int32, (8, LANES), 0)
    tally = jnp.zeros((8, LANES), F32)
    for s in range(steps):
        ids = jnp.broadcast_to(doc_ids[0, s:s + 1, :].astype(F32), (tokens, tokens))
        ids = jnp.sum(jnp.where(eye, ids, 0.0), axis=1, keepdims=True)
        onehot = (ids == lane).astype(F32)
        onehots.append(onehot)
        tally = tally + jnp.where(row8 == s, jnp.sum(onehot, axis=0, keepdims=True), 0.0)
    counts[me] = tally

    barrier = pltpu.get_barrier_semaphore()
    for j in others:
        pl.semaphore_signal(barrier, inc=1, device_id=(rep, j), device_id_type=MESH)
    for i in peers:
        pl.semaphore_signal(barrier, inc=1, device_id=(i, me), device_id_type=MESH)
    pl.semaphore_wait(barrier, n + replicas - 2)

    def to_all(buf, send, recv, j):
        return pltpu.make_async_remote_copy(
            src_ref=buf.at[me], dst_ref=buf.at[me], send_sem=send.at[j], recv_sem=recv.at[me],
            device_id=(rep, j), device_id_type=MESH)

    def from_all(buf, send, recv, j):
        pltpu.make_async_remote_copy(
            src_ref=buf.at[j], dst_ref=buf.at[j], send_sem=send.at[j], recv_sem=recv.at[j],
            device_id=(rep, j), device_id_type=MESH).wait_recv()

    for j in others:
        to_all(counts, count_send, count_recv, j).start()

    def a2a(u, j):
        return pltpu.make_async_remote_copy(
            src_ref=held_tokens(u, j), dst_ref=cols.at[u, my_tokens, :],
            send_sem=a2a_send.at[u, j], recv_sem=a2a_recv.at[u, me],
            device_id=(rep, j), device_id_type=MESH)

    def a2a_arrived(u, j):
        pltpu.make_async_remote_copy(
            src_ref=held_tokens(u, j), dst_ref=cols.at[u, block(slot(j), few), :],
            send_sem=a2a_send.at[u, j], recv_sem=a2a_recv.at[u, j],
            device_id=(rep, j), device_id_type=MESH).wait_recv()

    for u in range(parts):
        for j in others:
            a2a(u, j).start()


    local[0].wait()
    picked = fragment[0]
    for k in range(width // fw):
        piece = w_ref[:, k * fw:(k + 1) * fw]
        if k == 0:
            frag_cols[...] = piece
        else:
            frag_cols[...] = jnp.where(picked == k, piece, frag_cols[...])

    def frag_copy(i):
        return pltpu.make_async_remote_copy(
            src_ref=frag_cols.at[block(i, own), :], dst_ref=frag_recv.at[rep],
            send_sem=frag_send.at[i], recv_sem=frag_got.at[rep],
            device_id=(i, me), device_id_type=MESH)

    for i in peers:
        frag_copy(i).start()
    frag_recv[rep] = frag_cols[my_frag, :]

    local[1].wait()
    wide = 4 * LANES
    for s in range(steps):
        def add_squares(c, acc, s=s):
            x = hid[s, :, block(c, wide)].astype(F32)
            return acc + x * x
        acc = lax.fori_loop(0, model // wide, add_squares, jnp.zeros((tokens, wide), F32))
        power = jnp.sum(acc, axis=1, keepdims=True) / model
        row_scale[s] = jnp.broadcast_to(lax.rsqrt(power + NORM_EPS), (tokens, LANES))

    for j in others:
        from_all(counts, count_send, count_recv, j)
    total = counts[0]
    for j in range(1, n):
        total = total + counts[j]
    inverse = jnp.where(total > 0.0, 1.0 / (DOCS * jnp.maximum(total, 1.0)), 0.0)
    for s in range(steps):
        weight = jnp.sum(onehots[s] * inverse[s:s + 1, :], axis=1, keepdims=True)
        token_weight[s] = jnp.broadcast_to(weight, (tokens, LANES))

    def across():
        return pltpu.make_async_remote_copy(
            src_ref=coef_mine, dst_ref=coef_got, send_sem=coef_sem.at[0], recv_sem=coef_sem.at[1],
            device_id=(rep, lax.rem(me + 2, n)), device_id_type=MESH)

    if paired:
        lines = jnp.zeros((8, LANES), F32)
        for s in range(steps):
            coef = token_weight[s] * row_scale[s] * row_scale[s] * (scale / width)
            line = jnp.sum(jnp.where(wide_eye, coef, 0.0), axis=0, keepdims=True)
            lines = lines + jnp.where(row8 == s, line, 0.0)
        coef_mine[...] = lines
        across().start()

    local[6 + units].wait()

    def part_copy(u, j):
        return pltpu.make_async_remote_copy(
            src_ref=part_send.at[u, block(j, few), :], dst_ref=part_recv.at[u, my_tokens, :],
            send_sem=part_send_sem.at[u, j], recv_sem=part_recv_sem.at[u, me],
            device_id=(rep, j), device_id_type=MESH)

    def grad_rows(u, first_row, size):
        start = u % parts * together + first_row * size
        return grads.at[u // parts, pl.ds(pl.multiple_of(start, size), size), :]

    def grad_copy(u, j):
        mine = grad_rows(u, me, few)
        return pltpu.make_async_remote_copy(
            src_ref=mine, dst_ref=mine, send_sem=grad_send.at[u, j],
            recv_sem=grad_recv.at[u, me], device_id=(rep, j), device_id_type=MESH)

    side, half = lax.rem(me, 2), me // 2
    mate, cross = me + 1 - 2 * side, lax.rem(me + 2, n)
    my_side, mate_side = block(side, 2 * few), block(1 - side, 2 * few)

    def pair_copy(kind, u):
        if kind == 0:
            src, dst, to = part_send.at[u, mate_side, :], part_recv.at[u, 0:2 * few, :], mate
        elif kind == 1:
            src, dst, to = part_send.at[u, my_side, :], part_recv.at[u, 2 * few:4 * few, :], cross
        else:
            src = dst = grad_rows(u, side, 2 * few)
            to = mate
        return pltpu.make_async_remote_copy(
            src_ref=src, dst_ref=dst, send_sem=part_send_sem.at[u, kind],
            recv_sem=part_recv_sem.at[u, kind], device_id=(rep, to), device_id_type=MESH)

    def pair_back(u):
        theirs = grad_rows(u, 1 - side, 2 * few)
        pltpu.make_async_remote_copy(
            src_ref=theirs, dst_ref=theirs, send_sem=part_send_sem.at[u, 2],
            recv_sem=part_recv_sem.at[u, 2], device_id=(rep, mate),
            device_id_type=MESH).wait_recv()

    tile = 256

    def factors(u):
        s, q = u // parts, u % parts
        few_rows = slice(q * few, (q + 1) * few)
        gain = row_scale[s, few_rows, :][:, :1]
        weight = token_weight[s, few_rows, :][:, :1]
        return s, q, few_rows, gain, weight

    def project(u, held):
        s, q = u // parts, u % parts
        for j in others:
            a2a_arrived(u, j)
        local[6 + u].wait()

        @pl.loop(0, width // tile)
        def _(c):
            at = block(c, tile)
            out = jnp.dot(cols[u], held[:, at], preferred_element_type=F32)
            partial[u, :, at] = out
            part_send[u, :, at] = out.astype(BF16)

        if paired:
            pair_copy(0, u).start()
        else:
            for j in others:
                part_copy(u, j).start()

        @pl.loop(0, rows // tile)
        def _(c):
            at = block(c, tile)
            turned[s, at, q * together:(q + 1) * together] = cols[u, :, at].T

    def join_mate(u):
        if not paired:
            return
        s, q, few_rows, gain, weight = factors(u)
        share = weight * gain / width
        goal = targets[0, s, few_rows, :].astype(F32)
        mine, theirs = block(half, few), block(1 - half, few)
        other_rows = block(slot(cross), few)
        pair_copy(0, u).wait_recv()
        near = partial[u, my_tokens, :] + part_recv[u, mine, :].astype(F32)
        near = near * (share * gain * scale) - share * goal
        far = partial[u, other_rows, :] + part_recv[u, theirs, :].astype(F32)
        far = far * coef_across[s, few_rows, :][:, :1]
        part_send[u, my_tokens, :] = near.astype(BF16)
        part_send[u, other_rows, :] = far.astype(BF16)
        pair_copy(1, u).start()
        partial[u, my_tokens, :] = near
        partial[u, other_rows, :] = far

    def join_across(u):
        s, q, few_rows, gain, weight = factors(u)
        start = q * together
        if paired:
            share = weight * gain / width
            other_rows = block(slot(cross), few)
            base = 2 * few
            pair_copy(1, u).wait_recv()
            near = partial[u, my_tokens, :] + part_recv[
                u, pl.ds(pl.multiple_of(base + half * few, few), few), :].astype(F32)
            far = partial[u, other_rows, :] + part_recv[
                u, pl.ds(pl.multiple_of(base + (1 - half) * few, few), few), :].astype(F32)
            grads[s, pl.ds(pl.multiple_of(start + slot(me) * few, few), few), :] = near.astype(BF16)
            grads[s, pl.ds(pl.multiple_of(start + slot(cross) * few, few), few), :] = far.astype(BF16)
            pair_copy(2, u).start()
            error = near / share
        else:
            values = partial[u, my_tokens, :]
            for j in others:
                at = block(j, few)
                pltpu.make_async_remote_copy(
                    src_ref=part_recv.at[u, at, :], dst_ref=part_recv.at[u, at, :],
                    send_sem=part_send_sem.at[u, j], recv_sem=part_recv_sem.at[u, j],
                    device_id=(rep, j), device_id_type=MESH).wait_recv()
                values = values + part_recv[u, at, :].astype(F32)
            error = values * (gain * scale) - targets[0, s, few_rows, :].astype(F32)
            grads[s, pl.ds(pl.multiple_of(start + me * few, few), few), :] = (
                (weight * gain / width) * error).astype(BF16)
            for j in others:
                grad_copy(u, j).start()
        loss = jnp.sum(weight * 0.5 * jnp.mean(error * error, axis=-1, keepdims=True))
        loss = jnp.where(row8 == s, loss, 0.0)
        if u == 0:
            losses[me] = loss
        else:
            losses[me] = losses[me] + loss
        if u == units - 1:
            for j in others:
                to_all(losses, loss_send, loss_recv, j).start()

    def join_all(u):
        if paired:
            pair_back(u)
        else:
            for j in others:
                theirs = grad_rows(u, j, few)
                pltpu.make_async_remote_copy(
                    src_ref=theirs, dst_ref=theirs, send_sem=grad_send.at[u, j],
                    recv_sem=grad_recv.at[u, j], device_id=(rep, j),
                    device_id_type=MESH).wait_recv()

    now, later = range(parts), range(parts, units)
    queue = [(u, j) for u in later for j in others]
    project(0, w_ref)
    for u in now:
        for j in others:
            a2a(u, j).wait_send()
    a2a(*queue[0]).start()
    for u in now[1:]:
        project(u, w_ref)
    if paired:
        across().wait_recv()
        for s in range(steps):
            line = jnp.broadcast_to(coef_got[s:s + 1, :], (tokens, LANES))
            column = jnp.sum(jnp.where(wide_eye, line, 0.0), axis=1, keepdims=True)
            coef_across[s] = jnp.broadcast_to(column, (tokens, LANES))
    for u in now:
        join_mate(u)
    a2a(*queue[1]).start()

    for i in peers:
        pltpu.make_async_remote_copy(
            src_ref=frag_recv.at[i], dst_ref=frag_recv.at[i], send_sem=frag_send.at[i],
            recv_sem=frag_got.at[i], device_id=(i, me), device_id_type=MESH).wait_recv()
    local[2].wait()
    local[3].wait()
    base = anchor_ref[...].astype(F32)
    delta = base - frag_recv[0].astype(F32)
    for i in range(1, replicas):
        delta = delta + (base - frag_recv[i].astype(F32))
    mean_delta = delta / replicas
    new_moment = NESTEROV * moment_ref[...].astype(F32) + mean_delta
    frag_all[my_frag, :] = base - OUTER_RATE * (mean_delta + NESTEROV * new_moment)

    def all_copy(i):
        return pltpu.make_async_remote_copy(
            src_ref=frag_all.at[my_frag, :], dst_ref=frag_all.at[my_frag, :],
            send_sem=all_send.at[i], recv_sem=all_got.at[rep],
            device_id=(i, me), device_id_type=MESH)

    for i in peers:
        all_copy(i).start()

    for u in now:
        join_across(u)
    for u, j in queue[2:]:
        a2a(u, j).start()
    for u in now:
        join_all(u)
    local[4].wait()
    local[5].wait()
    rt = 128

    @pl.loop(0, rows // rt)
    def _(c):
        at = block(c, rt)
        gradient = jnp.dot(turned[0, at, :], grads[0], preferred_element_type=F32) * scale
        new_master, new_first, new_second = adam_update(
            w_ref[at, :].astype(F32), m_ref[at, :].astype(F32), v_ref[at, :].astype(F32), gradient)
        current[at, :] = new_master.astype(BF16)
        first[at, :] = (INNER_RATE * BETA_FIRST) * new_first
        second[at, :] = BETA_SECOND * new_second
        master[at, :] = (1.0 - INNER_RATE * DECAY_RATE) * new_master

    def mix():
        for i in peers:
            at = block(i, own)
            pltpu.make_async_remote_copy(
                src_ref=frag_all.at[at, :], dst_ref=frag_all.at[at, :], send_sem=all_send.at[i],
                recv_sem=all_got.at[i], device_id=(i, me), device_id_type=MESH).wait_recv()

        @pl.loop(0, rows // rt)
        def _(c):
            at = block(c, rt)
            mixed = (1.0 - MIXING) * frag_all[at, :]
            for k in range(width // fw):
                piece = master[at, k * fw:(k + 1) * fw]
                master[at, k * fw:(k + 1) * fw] = jnp.where(
                    picked == k, MIXING * piece + mixed, piece)

    stages = [lambda u: project(u, current), join_mate, join_across, join_all]
    for turn in range(2 * (parts - 1) + len(stages)):
        for i, u in reversed(list(enumerate(later))):
            if 0 <= turn - 2 * i < len(stages):
                stages[turn - 2 * i](u)
        if turn == 0:
            mix()
    for j in others:
        from_all(losses, loss_send, loss_recv, j)
    loss = losses[0]
    for j in range(1, n):
        loss = loss + losses[j]
    loss_out[...] = loss

    for j in others:
        for u in range(parts, units):
            a2a(u, j).wait_send()
        to_all(counts, count_send, count_recv, j).wait_send()
        to_all(losses, loss_send, loss_recv, j).wait_send()
        if not paired:
            for u in range(units):
                part_copy(u, j).wait_send()
                grad_copy(u, j).wait_send()
    if paired:
        across().wait_send()
        for u in range(units):
            for kind in range(3):
                pair_copy(kind, u).wait_send()
    for i in peers:
        frag_copy(i).wait_send()
        all_copy(i).wait_send()


def finish_kernel(scale, fw, fragment, kept, first, second, turned, grads, loss, out, loss_out,
                  done, out_sem):
    rows, width = kept.shape
    last = turned.shape[0] - 1
    tiles = out_sem.shape[0]
    rt = rows // tiles
    column = lax.broadcasted_iota(jnp.int32, (1, width), 1) // fw
    share = jnp.where(column == fragment[0], MIXING, 1.0)

    def write(c):
        at = pl.ds(pl.multiple_of(c * rt, rt), rt)
        return pltpu.make_async_copy(done.at[at, :], out.at[0, at, :], out_sem.at[c])

    @pl.loop(0, tiles)
    def _(c):
        at = pl.ds(pl.multiple_of(c * rt, rt), rt)
        raw = jnp.dot(turned[last, at, :], grads[last], preferred_element_type=F32)
        moved = first[at, :] + (INNER_RATE * (1.0 - BETA_FIRST) * scale) * raw
        power = second[at, :] + ((1.0 - BETA_SECOND) * scale * scale) * (raw * raw)
        step = moved / (power * lax.rsqrt(power) + ADAM_EPS)
        done[at, :] = kept[at, :] - share * step
        write(c).start()

    steps = loss_out.shape[1]
    across = lax.broadcasted_iota(jnp.int32, (1, steps), 1)
    line = jnp.zeros((1, steps), F32)
    for s in range(steps):
        line = jnp.where(across == s, loss[s:s + 1, :steps], line)
    loss_out[...] = line

    @pl.loop(0, tiles)
    def _(c):
        write(c).wait()


def body(n, replicas, hidden, targets, doc_ids, weights, adam_m, adam_v, anchor, momentum, fragment):
    steps, tokens, model = hidden.shape[1:]
    rows, width = weights.shape[1:]
    fw = anchor.shape[1]
    own = rows // replicas
    everyone = n * tokens
    parts = 2 if tokens % 32 == 0 else 1
    units = steps * parts
    together = everyone // parts
    dims = (steps, tokens, rows, width, model, fw)
    any_spec = pl.BlockSpec(memory_space=pltpu.HBM)
    vmem = pl.BlockSpec(memory_space=pltpu.VMEM)
    smem = pl.BlockSpec(memory_space=pltpu.SMEM)
    dma = pltpu.SemaphoreType.DMA
    shape = jax.ShapeDtypeStruct
    outer = [pltpu.with_memory_space_constraint(x, pltpu.HBM) for x in (
        hidden, targets, doc_ids, weights, adam_m, adam_v, anchor, momentum)]
    master, first, second, turned, grads, loss = pl.pallas_call(
        functools.partial(window_kernel, n, replicas, dims),
        out_shape=[
            pltpu.VMEM((rows, width), F32), pltpu.VMEM((rows, width), F32),
            pltpu.VMEM((rows, width), F32), pltpu.VMEM((steps, rows, everyone), BF16),
            pltpu.VMEM((steps, everyone, width), BF16), pltpu.VMEM((8, LANES), F32),
        ],
        in_specs=[any_spec] * 8 + [smem],
        out_specs=[vmem] * 6,
        scratch_shapes=[
            pltpu.VMEM((units, together, rows), BF16),
            pltpu.VMEM((steps, tokens, model), BF16),
            pltpu.VMEM((1, steps, tokens, width), BF16),
            pltpu.VMEM((1, steps, tokens), jnp.int32),
            pltpu.VMEM((rows, width), BF16),
            pltpu.VMEM((rows, width), BF16),
            pltpu.VMEM((rows, width), BF16),
            pltpu.VMEM((rows, width), BF16),
            pltpu.VMEM((units, together, width), F32),
            pltpu.VMEM((units, together, width), BF16),
            pltpu.VMEM((units, together, width), BF16),
            pltpu.VMEM((n, 8, LANES), F32),
            pltpu.VMEM((n, 8, LANES), F32),
            pltpu.VMEM((rows, fw), BF16),
            pltpu.VMEM((replicas, own, fw), BF16),
            pltpu.VMEM((rows, fw), F32),
            pltpu.VMEM((own, fw), BF16),
            pltpu.VMEM((own, fw), BF16),
            pltpu.VMEM((steps, tokens, LANES), F32),
            pltpu.VMEM((steps, tokens, LANES), F32),
            pltpu.VMEM((8, LANES), F32),
            pltpu.VMEM((8, LANES), F32),
            pltpu.VMEM((steps, tokens, LANES), F32),
            dma((2,)),
            dma((8 + units,)),
            dma((units, n)), dma((units, n)), dma((n,)), dma((n,)),
            dma((replicas,)), dma((replicas,)), dma((replicas,)), dma((replicas,)),
            dma((units, n)), dma((units, n)),
            dma((units, n)), dma((units, n)), dma((n,)), dma((n,)),
        ],
        compiler_params=pltpu.CompilerParams(
            collective_id=0, has_side_effects=True, vmem_limit_bytes=28 * 1024 * 1024),
        name="window",
    )(*outer, fragment)

    inner = [pltpu.with_memory_space_constraint(x, pltpu.VMEM)
             for x in (master, first, second, turned, grads, loss)]
    return pl.pallas_call(
        functools.partial(finish_kernel, model ** (-0.5), fw),
        out_shape=[shape((1, rows, width), F32), shape((1, steps), F32)],
        in_specs=[smem] + [vmem] * 6,
        out_specs=[any_spec, vmem],
        scratch_shapes=[pltpu.VMEM((rows, width), F32), dma((8,))],
        compiler_params=pltpu.CompilerParams(vmem_limit_bytes=16 * 1024 * 1024),
        name="finish",
    )(fragment, *inner)


def solution(mesh):
    placed = (
        P("replica", None, "fsdp", None),
        P("replica", None, "fsdp", None),
        P("replica", None, "fsdp"),
        P("replica", "fsdp", None),
        P("replica", "fsdp", None),
        P("replica", "fsdp", None),
        P("fsdp", None),
        P("fsdp", None),
        P(),
    )
    return jax.shard_map(
        functools.partial(body, mesh.shape["fsdp"], mesh.shape["replica"]),
        mesh=mesh,
        in_specs=placed,
        out_specs=(P("replica", "fsdp", None), P("replica", None)),
        check_vma=False,
    )
```

```python
import functools

import jax
import jax.numpy as jnp
from jax import lax
from jax.experimental import pallas as pl
from jax.experimental.pallas import tpu as pltpu
from jax.sharding import PartitionSpec as P

DOCS = 8
NORM_EPS = 1e-05
ADAM_EPS = 1e-08
INNER_RATE = 0.1
DECAY_RATE = 0.1
BETA_FIRST = 0.9
BETA_SECOND = 0.95
OUTER_RATE = 0.7
NESTEROV = 0.9
MIXING = 0.5
LANES = 128
MESH = pl.DeviceIdType.MESH
F32 = jnp.float32
BF16 = jnp.bfloat16


def adam_update(master, first, second, gradient):
    first = BETA_FIRST * first + (1.0 - BETA_FIRST) * gradient
    second = BETA_SECOND * second + (1.0 - BETA_SECOND) * gradient * gradient
    master = master - INNER_RATE * (first / (second * lax.rsqrt(second) + ADAM_EPS) + DECAY_RATE * master)
    return (master, first, second)


def partners(me, n):
    if n == 4:
        return [lax.rem(me + 2, 4), 3 - me, me + 1 - 2 * lax.rem(me, 2)]
    return [lax.rem(me + k, n) for k in range(1, n)]


def window_kernel(
    n, replicas, dims,
    hidden, targets_in, ids_in, weights, adam_m, adam_v, anchor, momentum, fragment,
    master, first, second, turned, grads, loss_out,
    cols, hid, targets, doc_ids, w_ref, m_ref, v_ref, current,
    partial, part_send, part_recv, counts, losses,
    frag_cols, frag_recv, frag_all, anchor_ref, moment_ref, row_scale, token_weight,
    coef_mine, coef_got, coef_across, coef_sem,
    local_sem, a2a_send, a2a_recv, count_send, count_recv,
    frag_send, frag_got, all_send, all_got, part_send_sem, part_recv_sem,
    grad_send, grad_recv, loss_send, loss_recv,
):
    steps, tokens, rows, width, model, fw = dims
    paired = n == 4 and tokens <= LANES
    units = cols.shape[0]
    parts = units // steps
    few = tokens // parts
    together = n * few
    own = rows // replicas
    scale = model ** (-0.5)
    rep = lax.axis_index("replica")
    me = lax.axis_index("fsdp")
    others = partners(me, n)
    peers = [lax.rem(rep + k, replicas) for k in range(1, replicas)]

    def block(index, size):
        return pl.ds(pl.multiple_of(index * size, size), size)

    def slot(j):
        return 2 * lax.rem(j, 2) + j // 2 if paired else j

    my_tokens = block(slot(me), few)
    my_frag = block(rep, own)

    local = [
        pltpu.make_async_copy(weights.at[0], w_ref, local_sem.at[0]),
        pltpu.make_async_copy(hidden.at[0], hid, local_sem.at[1]),
        pltpu.make_async_copy(anchor.at[my_frag, :], anchor_ref, local_sem.at[2]),
        pltpu.make_async_copy(momentum.at[my_frag, :], moment_ref, local_sem.at[3]),
        pltpu.make_async_copy(adam_m.at[0], m_ref, local_sem.at[4]),
        pltpu.make_async_copy(adam_v.at[0], v_ref, local_sem.at[5]),
    ]

    def held_tokens(u, j):
        return hidden.at[0, u // parts, u % parts * few:(u % parts + 1) * few, block(j, rows)]

    for u in range(units):
        local.append(pltpu.make_async_copy(
            held_tokens(u, me), cols.at[u, my_tokens, :], local_sem.at[6 + u]))
    local.append(pltpu.make_async_copy(targets_in, targets, local_sem.at[6 + units]))
    local.append(pltpu.make_async_copy(ids_in, doc_ids, local_sem.at[7 + units]))
    for copy in local:
        copy.start()

    local[7 + units].wait()
    lane = lax.broadcasted_iota(jnp.int32, (tokens, LANES), 1).astype(F32)
    eye = (lax.broadcasted_iota(jnp.int32, (tokens, tokens), 0)
           == lax.broadcasted_iota(jnp.int32, (tokens, tokens), 1))
    wide_eye = (lax.broadcasted_iota(jnp.int32, (tokens, LANES), 0)
                == lax.broadcasted_iota(jnp.int32, (tokens, LANES), 1))
    onehots = []
    row8 = lax.broadcasted_iota(jnp.int32, (8, LANES), 0)
    tally = jnp.zeros((8, LANES), F32)
    for s in range(steps):
        ids = jnp.broadcast_to(doc_ids[0, s:s + 1, :].astype(F32), (tokens, tokens))
        ids = jnp.sum(jnp.where(eye, ids, 0.0), axis=1, keepdims=True)
        onehot = (ids == lane).astype(F32)
        onehots.append(onehot)
        tally = tally + jnp.where(row8 == s, jnp.sum(onehot, axis=0, keepdims=True), 0.0)
    counts[me] = tally

    barrier = pltpu.get_barrier_semaphore()
    for j in others:
        pl.semaphore_signal(barrier, inc=1, device_id=(rep, j), device_id_type=MESH)
    for i in peers:
        pl.semaphore_signal(barrier, inc=1, device_id=(i, me), device_id_type=MESH)
    pl.semaphore_wait(barrier, n + replicas - 2)

    def to_all(buf, send, recv, j):
        return pltpu.make_async_remote_copy(
            src_ref=buf.at[me], dst_ref=buf.at[me], send_sem=send.at[j], recv_sem=recv.at[me],
            device_id=(rep, j), device_id_type=MESH)

    def from_all(buf, send, recv, j):
        pltpu.make_async_remote_copy(
            src_ref=buf.at[j], dst_ref=buf.at[j], send_sem=send.at[j], recv_sem=recv.at[j],
            device_id=(rep, j), device_id_type=MESH).wait_recv()

    for j in others:
        to_all(counts, count_send, count_recv, j).start()

    def a2a(u, j):
        return pltpu.make_async_remote_copy(
            src_ref=held_tokens(u, j), dst_ref=cols.at[u, my_tokens, :],
            send_sem=a2a_send.at[u, j], recv_sem=a2a_recv.at[u, me],
            device_id=(rep, j), device_id_type=MESH)

    def a2a_arrived(u, j):
        pltpu.make_async_remote_copy(
            src_ref=held_tokens(u, j), dst_ref=cols.at[u, block(slot(j), few), :],
            send_sem=a2a_send.at[u, j], recv_sem=a2a_recv.at[u, j],
            device_id=(rep, j), device_id_type=MESH).wait_recv()

    for u in range(parts):
        for j in others:
            a2a(u, j).start()


    local[0].wait()
    picked = fragment[0]
    for k in range(width // fw):
        piece = w_ref[:, k * fw:(k + 1) * fw]
        if k == 0:
            frag_cols[...] = piece
        else:
            frag_cols[...] = jnp.where(picked == k, piece, frag_cols[...])

    def frag_copy(i):
        return pltpu.make_async_remote_copy(
            src_ref=frag_cols.at[block(i, own), :], dst_ref=frag_recv.at[rep],
            send_sem=frag_send.at[i], recv_sem=frag_got.at[rep],
            device_id=(i, me), device_id_type=MESH)

    for i in peers:
        frag_copy(i).start()
    frag_recv[rep] = frag_cols[my_frag, :]

    local[1].wait()
    wide = 4 * LANES
    for s in range(steps):
        def add_squares(c, acc, s=s):
            x = hid[s, :, block(c, wide)].astype(F32)
            return acc + x * x
        acc = lax.fori_loop(0, model // wide, add_squares, jnp.zeros((tokens, wide), F32))
        power = jnp.sum(acc, axis=1, keepdims=True) / model
        row_scale[s] = jnp.broadcast_to(lax.rsqrt(power + NORM_EPS), (tokens, LANES))

    for j in others:
        from_all(counts, count_send, count_recv, j)
    total = counts[0]
    for j in range(1, n):
        total = total + counts[j]
    inverse = jnp.where(total > 0.0, 1.0 / (DOCS * jnp.maximum(total, 1.0)), 0.0)
    for s in range(steps):
        weight = jnp.sum(onehots[s] * inverse[s:s + 1, :], axis=1, keepdims=True)
        token_weight[s] = jnp.broadcast_to(weight, (tokens, LANES))

    def across():
        return pltpu.make_async_remote_copy(
            src_ref=coef_mine, dst_ref=coef_got, send_sem=coef_sem.at[0], recv_sem=coef_sem.at[1],
            device_id=(rep, lax.rem(me + 2, n)), device_id_type=MESH)

    if paired:
        lines = jnp.zeros((8, LANES), F32)
        for s in range(steps):
            coef = token_weight[s] * row_scale[s] * row_scale[s] * (scale / width)
            line = jnp.sum(jnp.where(wide_eye, coef, 0.0), axis=0, keepdims=True)
            lines = lines + jnp.where(row8 == s, line, 0.0)
        coef_mine[...] = lines
        across().start()

    local[6 + units].wait()

    def part_copy(u, j):
        return pltpu.make_async_remote_copy(
            src_ref=part_send.at[u, block(j, few), :], dst_ref=part_recv.at[u, my_tokens, :],
            send_sem=part_send_sem.at[u, j], recv_sem=part_recv_sem.at[u, me],
            device_id=(rep, j), device_id_type=MESH)

    def grad_rows(u, first_row, size):
        start = u % parts * together + first_row * size
        return grads.at[u // parts, pl.ds(pl.multiple_of(start, size), size), :]

    def grad_copy(u, j):
        mine = grad_rows(u, me, few)
        return pltpu.make_async_remote_copy(
            src_ref=mine, dst_ref=mine, send_sem=grad_send.at[u, j],
            recv_sem=grad_recv.at[u, me], device_id=(rep, j), device_id_type=MESH)

    side, half = lax.rem(me, 2), me // 2
    mate, cross = me + 1 - 2 * side, lax.rem(me + 2, n)
    my_side, mate_side = block(side, 2 * few), block(1 - side, 2 * few)

    def pair_copy(kind, u):
        if kind == 0:
            src, dst, to = part_send.at[u, mate_side, :], part_recv.at[u, 0:2 * few, :], mate
        elif kind == 1:
            src, dst, to = part_send.at[u, my_side, :], part_recv.at[u, 2 * few:4 * few, :], cross
        else:
            src = dst = grad_rows(u, side, 2 * few)
            to = mate
        return pltpu.make_async_remote_copy(
            src_ref=src, dst_ref=dst, send_sem=part_send_sem.at[u, kind],
            recv_sem=part_recv_sem.at[u, kind], device_id=(rep, to), device_id_type=MESH)

    def pair_back(u):
        theirs = grad_rows(u, 1 - side, 2 * few)
        pltpu.make_async_remote_copy(
            src_ref=theirs, dst_ref=theirs, send_sem=part_send_sem.at[u, 2],
            recv_sem=part_recv_sem.at[u, 2], device_id=(rep, mate),
            device_id_type=MESH).wait_recv()

    tile = 256

    def factors(u):
        s, q = u // parts, u % parts
        few_rows = slice(q * few, (q + 1) * few)
        gain = row_scale[s, few_rows, :][:, :1]
        weight = token_weight[s, few_rows, :][:, :1]
        return s, q, few_rows, gain, weight

    def project(u, held):
        s, q = u // parts, u % parts
        for j in others:
            a2a_arrived(u, j)
        local[6 + u].wait()

        @pl.loop(0, width // tile)
        def _(c):
            at = block(c, tile)
            out = jnp.dot(cols[u], held[:, at], preferred_element_type=F32)
            partial[u, :, at] = out
            part_send[u, :, at] = out.astype(BF16)

        if paired:
            pair_copy(0, u).start()
        else:
            for j in others:
                part_copy(u, j).start()

        @pl.loop(0, rows // tile)
        def _(c):
            at = block(c, tile)
            turned[s, at, q * together:(q + 1) * together] = cols[u, :, at].T

    def join_mate(u):
        if not paired:
            return
        s, q, few_rows, gain, weight = factors(u)
        share = weight * gain / width
        goal = targets[0, s, few_rows, :].astype(F32)
        mine, theirs = block(half, few), block(1 - half, few)
        other_rows = block(slot(cross), few)
        pair_copy(0, u).wait_recv()
        near = partial[u, my_tokens, :] + part_recv[u, mine, :].astype(F32)
        near = near * (share * gain * scale) - share * goal
        far = partial[u, other_rows, :] + part_recv[u, theirs, :].astype(F32)
        far = far * coef_across[s, few_rows, :][:, :1]
        part_send[u, my_tokens, :] = near.astype(BF16)
        part_send[u, other_rows, :] = far.astype(BF16)
        pair_copy(1, u).start()
        partial[u, my_tokens, :] = near
        partial[u, other_rows, :] = far

    def join_across(u):
        s, q, few_rows, gain, weight = factors(u)
        start = q * together
        if paired:
            share = weight * gain / width
            other_rows = block(slot(cross), few)
            base = 2 * few
            pair_copy(1, u).wait_recv()
            near = partial[u, my_tokens, :] + part_recv[
                u, pl.ds(pl.multiple_of(base + half * few, few), few), :].astype(F32)
            far = partial[u, other_rows, :] + part_recv[
                u, pl.ds(pl.multiple_of(base + (1 - half) * few, few), few), :].astype(F32)
            grads[s, pl.ds(pl.multiple_of(start + slot(me) * few, few), few), :] = near.astype(BF16)
            grads[s, pl.ds(pl.multiple_of(start + slot(cross) * few, few), few), :] = far.astype(BF16)
            pair_copy(2, u).start()
            error = near / share
        else:
            values = partial[u, my_tokens, :]
            for j in others:
                at = block(j, few)
                pltpu.make_async_remote_copy(
                    src_ref=part_recv.at[u, at, :], dst_ref=part_recv.at[u, at, :],
                    send_sem=part_send_sem.at[u, j], recv_sem=part_recv_sem.at[u, j],
                    device_id=(rep, j), device_id_type=MESH).wait_recv()
                values = values + part_recv[u, at, :].astype(F32)
            error = values * (gain * scale) - targets[0, s, few_rows, :].astype(F32)
            grads[s, pl.ds(pl.multiple_of(start + me * few, few), few), :] = (
                (weight * gain / width) * error).astype(BF16)
            for j in others:
                grad_copy(u, j).start()
        loss = jnp.sum(weight * 0.5 * jnp.mean(error * error, axis=-1, keepdims=True))
        loss = jnp.where(row8 == s, loss, 0.0)
        if u == 0:
            losses[me] = loss
        else:
            losses[me] = losses[me] + loss
        if u == units - 1:
            for j in others:
                to_all(losses, loss_send, loss_recv, j).start()

    def join_all(u):
        if paired:
            pair_back(u)
        else:
            for j in others:
                theirs = grad_rows(u, j, few)
                pltpu.make_async_remote_copy(
                    src_ref=theirs, dst_ref=theirs, send_sem=grad_send.at[u, j],
                    recv_sem=grad_recv.at[u, j], device_id=(rep, j),
                    device_id_type=MESH).wait_recv()

    now, later = range(parts), range(parts, units)
    queue = [(u, j) for u in later for j in others]
    project(0, w_ref)
    a2a(now[-1], others[0]).wait_send()
    a2a(*queue[0]).start()
    for u in now[1:]:
        project(u, w_ref)
    if paired:
        across().wait_recv()
        for s in range(steps):
            line = jnp.broadcast_to(coef_got[s:s + 1, :], (tokens, LANES))
            column = jnp.sum(jnp.where(wide_eye, line, 0.0), axis=1, keepdims=True)
            coef_across[s] = jnp.broadcast_to(column, (tokens, LANES))
    for u in now:
        join_mate(u)
    a2a(*queue[1]).start()

    for i in peers:
        pltpu.make_async_remote_copy(
            src_ref=frag_recv.at[i], dst_ref=frag_recv.at[i], send_sem=frag_send.at[i],
            recv_sem=frag_got.at[i], device_id=(i, me), device_id_type=MESH).wait_recv()
    local[2].wait()
    local[3].wait()
    base = anchor_ref[...].astype(F32)
    delta = base - frag_recv[0].astype(F32)
    for i in range(1, replicas):
        delta = delta + (base - frag_recv[i].astype(F32))
    mean_delta = delta / replicas
    new_moment = NESTEROV * moment_ref[...].astype(F32) + mean_delta
    frag_all[my_frag, :] = base - OUTER_RATE * (mean_delta + NESTEROV * new_moment)

    def all_copy(i):
        return pltpu.make_async_remote_copy(
            src_ref=frag_all.at[my_frag, :], dst_ref=frag_all.at[my_frag, :],
            send_sem=all_send.at[i], recv_sem=all_got.at[rep],
            device_id=(i, me), device_id_type=MESH)

    for i in peers:
        all_copy(i).start()

    for u in now:
        join_across(u)
    for u, j in queue[2:]:
        a2a(u, j).start()
    for u in now:
        join_all(u)
    local[4].wait()
    local[5].wait()
    rt = 128

    @pl.loop(0, rows // rt)
    def _(c):
        at = block(c, rt)
        gradient = jnp.dot(turned[0, at, :], grads[0], preferred_element_type=F32) * scale
        new_master, new_first, new_second = adam_update(
            w_ref[at, :].astype(F32), m_ref[at, :].astype(F32), v_ref[at, :].astype(F32), gradient)
        current[at, :] = new_master.astype(BF16)
        first[at, :] = (INNER_RATE * BETA_FIRST) * new_first
        second[at, :] = BETA_SECOND * new_second
        master[at, :] = (1.0 - INNER_RATE * DECAY_RATE) * new_master

    def mix():
        for i in peers:
            at = block(i, own)
            pltpu.make_async_remote_copy(
                src_ref=frag_all.at[at, :], dst_ref=frag_all.at[at, :], send_sem=all_send.at[i],
                recv_sem=all_got.at[i], device_id=(i, me), device_id_type=MESH).wait_recv()

        @pl.loop(0, rows // rt)
        def _(c):
            at = block(c, rt)
            mixed = (1.0 - MIXING) * frag_all[at, :]
            for k in range(width // fw):
                piece = master[at, k * fw:(k + 1) * fw]
                master[at, k * fw:(k + 1) * fw] = jnp.where(
                    picked == k, MIXING * piece + mixed, piece)

    stages = [lambda u: project(u, current), join_mate, join_across, join_all]
    for turn in range(2 * (parts - 1) + len(stages)):
        for i, u in reversed(list(enumerate(later))):
            if 0 <= turn - 2 * i < len(stages):
                stages[turn - 2 * i](u)
        if turn == 0:
            mix()
    for j in others:
        from_all(losses, loss_send, loss_recv, j)
    loss = losses[0]
    for j in range(1, n):
        loss = loss + losses[j]
    loss_out[...] = loss

    for k, j in enumerate(others):
        for u in range(units):
            if (u, k) != (parts - 1, 0):
                a2a(u, j).wait_send()
        to_all(counts, count_send, count_recv, j).wait_send()
        to_all(losses, loss_send, loss_recv, j).wait_send()
        if not paired:
            for u in range(units):
                part_copy(u, j).wait_send()
                grad_copy(u, j).wait_send()
    if paired:
        across().wait_send()
        for u in range(units):
            for kind in range(3):
                pair_copy(kind, u).wait_send()
    for i in peers:
        frag_copy(i).wait_send()
        all_copy(i).wait_send()


def finish_kernel(scale, fw, fragment, kept, first, second, turned, grads, loss, out, loss_out,
                  done, out_sem):
    rows, width = kept.shape
    last = turned.shape[0] - 1
    tiles = out_sem.shape[0]
    rt = rows // tiles
    column = lax.broadcasted_iota(jnp.int32, (1, width), 1) // fw
    share = jnp.where(column == fragment[0], MIXING, 1.0)

    def write(c):
        at = pl.ds(pl.multiple_of(c * rt, rt), rt)
        return pltpu.make_async_copy(done.at[at, :], out.at[0, at, :], out_sem.at[c])

    @pl.loop(0, tiles)
    def _(c):
        at = pl.ds(pl.multiple_of(c * rt, rt), rt)
        raw = jnp.dot(turned[last, at, :], grads[last], preferred_element_type=F32)
        moved = first[at, :] + (INNER_RATE * (1.0 - BETA_FIRST) * scale) * raw
        power = second[at, :] + ((1.0 - BETA_SECOND) * scale * scale) * (raw * raw)
        step = moved / (power * lax.rsqrt(power) + ADAM_EPS)
        done[at, :] = kept[at, :] - share * step
        write(c).start()

    steps = loss_out.shape[1]
    across = lax.broadcasted_iota(jnp.int32, (1, steps), 1)
    line = jnp.zeros((1, steps), F32)
    for s in range(steps):
        line = jnp.where(across == s, loss[s:s + 1, :steps], line)
    loss_out[...] = line

    @pl.loop(0, tiles)
    def _(c):
        write(c).wait()


def body(n, replicas, hidden, targets, doc_ids, weights, adam_m, adam_v, anchor, momentum, fragment):
    steps, tokens, model = hidden.shape[1:]
    rows, width = weights.shape[1:]
    fw = anchor.shape[1]
    own = rows // replicas
    everyone = n * tokens
    parts = 2 if tokens % 32 == 0 else 1
    units = steps * parts
    together = everyone // parts
    dims = (steps, tokens, rows, width, model, fw)
    any_spec = pl.BlockSpec(memory_space=pltpu.HBM)
    vmem = pl.BlockSpec(memory_space=pltpu.VMEM)
    smem = pl.BlockSpec(memory_space=pltpu.SMEM)
    dma = pltpu.SemaphoreType.DMA
    shape = jax.ShapeDtypeStruct
    outer = [pltpu.with_memory_space_constraint(x, pltpu.HBM) for x in (
        hidden, targets, doc_ids, weights, adam_m, adam_v, anchor, momentum)]
    master, first, second, turned, grads, loss = pl.pallas_call(
        functools.partial(window_kernel, n, replicas, dims),
        out_shape=[
            pltpu.VMEM((rows, width), F32), pltpu.VMEM((rows, width), F32),
            pltpu.VMEM((rows, width), F32), pltpu.VMEM((steps, rows, everyone), BF16),
            pltpu.VMEM((steps, everyone, width), BF16), pltpu.VMEM((8, LANES), F32),
        ],
        in_specs=[any_spec] * 8 + [smem],
        out_specs=[vmem] * 6,
        scratch_shapes=[
            pltpu.VMEM((units, together, rows), BF16),
            pltpu.VMEM((steps, tokens, model), BF16),
            pltpu.VMEM((1, steps, tokens, width), BF16),
            pltpu.VMEM((1, steps, tokens), jnp.int32),
            pltpu.VMEM((rows, width), BF16),
            pltpu.VMEM((rows, width), BF16),
            pltpu.VMEM((rows, width), BF16),
            pltpu.VMEM((rows, width), BF16),
            pltpu.VMEM((units, together, width), F32),
            pltpu.VMEM((units, together, width), BF16),
            pltpu.VMEM((units, together, width), BF16),
            pltpu.VMEM((n, 8, LANES), F32),
            pltpu.VMEM((n, 8, LANES), F32),
            pltpu.VMEM((rows, fw), BF16),
            pltpu.VMEM((replicas, own, fw), BF16),
            pltpu.VMEM((rows, fw), F32),
            pltpu.VMEM((own, fw), BF16),
            pltpu.VMEM((own, fw), BF16),
            pltpu.VMEM((steps, tokens, LANES), F32),
            pltpu.VMEM((steps, tokens, LANES), F32),
            pltpu.VMEM((8, LANES), F32),
            pltpu.VMEM((8, LANES), F32),
            pltpu.VMEM((steps, tokens, LANES), F32),
            dma((2,)),
            dma((8 + units,)),
            dma((units, n)), dma((units, n)), dma((n,)), dma((n,)),
            dma((replicas,)), dma((replicas,)), dma((replicas,)), dma((replicas,)),
            dma((units, n)), dma((units, n)),
            dma((units, n)), dma((units, n)), dma((n,)), dma((n,)),
        ],
        compiler_params=pltpu.CompilerParams(
            collective_id=0, has_side_effects=True, vmem_limit_bytes=28 * 1024 * 1024),
        name="window",
    )(*outer, fragment)

    inner = [pltpu.with_memory_space_constraint(x, pltpu.VMEM)
             for x in (master, first, second, turned, grads, loss)]
    return pl.pallas_call(
        functools.partial(finish_kernel, model ** (-0.5), fw),
        out_shape=[shape((1, rows, width), F32), shape((1, steps), F32)],
        in_specs=[smem] + [vmem] * 6,
        out_specs=[any_spec, vmem],
        scratch_shapes=[pltpu.VMEM((rows, width), F32), dma((8,))],
        compiler_params=pltpu.CompilerParams(vmem_limit_bytes=16 * 1024 * 1024),
        name="finish",
    )(fragment, *inner)


def solution(mesh):
    placed = (
        P("replica", None, "fsdp", None),
        P("replica", None, "fsdp", None),
        P("replica", None, "fsdp"),
        P("replica", "fsdp", None),
        P("replica", "fsdp", None),
        P("replica", "fsdp", None),
        P("fsdp", None),
        P("fsdp", None),
        P(),
    )
    return jax.shard_map(
        functools.partial(body, mesh.shape["fsdp"], mesh.shape["replica"]),
        mesh=mesh,
        in_specs=placed,
        out_specs=(P("replica", "fsdp", None), P("replica", None)),
        check_vma=False,
    )
```
